256 devices in a mesh: gx: 4 (over y_hi, core), gy: 8 (over z), gz: 8 (over y_lo, x).
Axes of the slice: x: 4, y: 4 (y_hi: 2, y_lo: 2; y = y_hi * 2 + y_lo), z: 8, core: 2. Of those that a mesh axis runs over, the one named last changes fastest.
Arguments:
- grad_out: bfloat16 [1024, 16384], P(('gx', 'gy'), 'gz'), may hold values from -1.1953125 to 1.1953125
- grad_side: bfloat16 [1024, 16384], P(('gx', 'gy'), 'gz'), may hold values from -1.1953125 to 1.1953125
- attn_out: bfloat16 [1024, 8192], P(('gx', 'gz'), 'gy'), may hold values from -1.796875 to 1.796875
- gate_pre: bfloat16 [1024, 26624], P(('gx', 'gz'), 'gy'), may hold values from -6 to 6
- up_pre: bfloat16 [1024, 26624], P(('gx', 'gz'), 'gy'), may hold values from -6 to 6
- seg_ids: int32 [1024], replicated, may hold values from 0 to 7, never falling along the last dimension, each value on 1 to 256 neighbouring positions
- down_weight: bfloat16 [26624, 16384], P(('gy', 'gx'), 'gz'), may hold values from -0.0390625 to 0.0390625
- out_weight: bfloat16 [8192, 16384], P(('gy', 'gx'), 'gz'), may hold values from -0.0625 to 0.0625
Outputs:
- grad_gate: bfloat16 [1024, 26624], P(('gx', 'gz'), 'gy')
- grad_up: bfloat16 [1024, 26624], P(('gx', 'gz'), 'gy')
- grad_attn: bfloat16 [1024, 8192], P(('gx', 'gz'), 'gy')
- grad_down: bfloat16 [26624, 16384], P(('gy', 'gx'), 'gz')
- grad_outproj: bfloat16 [8192, 16384], P(('gy', 'gx'), 'gz')
The draws below stay inside these ranges and needn't reach their ends.
Inputs may be any that keep to these rules, and one draw needn't show every extreme that they name: `seg_ids`: each of 8 documents covers 1 to 256 consecutive tokens, ids never fall, and one document has exactly 256 tokens.
All inputs are finite; a program needn't handle non-finite values.
Results may differ from the reference program's by a relative error of at most 0.025.
Values may be sent and summed in bfloat16 or wider, within the bound.
A program may use at most 128 MiB of HBM per device.

```python
import math
import jax
import jax.numpy as jnp
import numpy as np
from jax import lax

D = 16384
FF = 26624
HD = 8192
TOKENS = 1024
NSEG = 8
SEG_MOST = 256
N_GX = 4
N_GZ = 8


def levels(rng, extent, cuts, smallest, largest):
    def one(axis_at, blocks):
        draws = jax.random.uniform(jax.random.fold_in(jax.random.fold_in(rng, 6), axis_at), (blocks,), jnp.float32, smallest / len(cuts), largest / len(cuts))
        return jnp.repeat(jnp.exp(draws), extent[axis_at] // blocks).reshape((-1,) + (1,) * (len(extent) - axis_at - 1))

    gain = one(*cuts[0])
    for cut in cuts[1:]:
        gain = gain * one(*cut)
    return gain


def length_profile(amount, total, limit, lean):
    portions = [(1 << 20) // math.isqrt(standing ** lean) + 1 for standing in range(2, amount + 1)]
    spare, holding = total - limit - (amount - 1), [1] * (amount - 1)
    while spare > 0:
        free = [i for i in range(amount - 1) if holding[i] < limit]
        pool, budget = sum([portions[i] for i in free]), spare
        for i in free:
            addition = min(limit - holding[i], max(1, budget * portions[i] // pool), spare)
            holding[i] = holding[i] + addition
            spare = spare - addition
    return np.array([limit] + holding)


def ragged(stream_key, number_of, total, limit, lean):
    if number_of == 2:
        one = jax.random.randint(stream_key, (), max(1, total - limit), min(limit, total - 1) + 1)
        return jnp.stack([one, total - one])
    tallies = jnp.asarray(length_profile(number_of, total, limit, lean), jnp.int32)
    twos = (number_of - 1) // 2
    giver, receiver = tallies[1:1 + 2 * twos:2], tallies[2:2 + 2 * twos:2]
    slack = jnp.minimum(giver - 1, limit - receiver)
    shifted = jax.random.randint(jax.random.fold_in(stream_key, 1), (twos,), 0, 1 << 20) % (slack + 1)
    tallies = tallies.at[1:1 + 2 * twos:2].set(giver - shifted).at[2:2 + 2 * twos:2].set(receiver + shifted)
    return tallies[jax.random.permutation(jax.random.fold_in(stream_key, 2), number_of)]


def normal_values(stream_key, extent, spread, bound, split=(), kind=jnp.bfloat16):
    gain = levels(stream_key, extent, split, -0.22, 0.18) if split else 1.0
    array = jax.random.normal(stream_key, extent, jnp.float32) * spread * gain
    return jnp.minimum(jnp.maximum(array, -bound), bound).astype(kind)


def setup_inputs(seed: int = 0) -> dict:
    key_of = jax.random.split(jax.random.key(seed), 9)
    return {
        "grad_out": normal_values(key_of[0], (TOKENS, D), 0.2, 1.1953125, ((0, 32), (1, 8))),
        "grad_side": normal_values(key_of[1], (TOKENS, D), 0.2, 1.1953125, ((0, 32), (1, 8))),
        "attn_out": normal_values(key_of[2], (TOKENS, HD), 0.3, 1.796875, ((0, 32), (1, 8))),
        "gate_pre": normal_values(key_of[3], (TOKENS, FF), 1.0, 6.0, ((0, 32), (1, 8))),
        "up_pre": normal_values(key_of[4], (TOKENS, FF), 1.0, 6.0, ((0, 32), (1, 8))),
        "seg_ids": jnp.searchsorted(jnp.cumsum(ragged(key_of[5], NSEG, TOKENS, SEG_MOST, 1)), jnp.arange(TOKENS), side="right").astype(jnp.int32),
        "down_weight": normal_values(key_of[6], (FF, D), FF ** -0.5, 0.0390625, ((0, 32), (1, 8))),
        "out_weight": normal_values(key_of[7], (HD, D), HD ** -0.5, 0.0625, ((0, 32), (1, 8))),
    }


def product_nt(lhs_mat, rhs_mat):
    return lax.dot_general(lhs_mat, rhs_mat, (((1,), (1,)), ((), ())), preferred_element_type=jnp.float32)


def product_tn(lhs_mat, rhs_mat):
    return lax.dot_general(lhs_mat, rhs_mat, (((0,), (0,)), ((), ())), preferred_element_type=jnp.float32)


def rounded(value):
    return lax.optimization_barrier(value.astype(jnp.bfloat16)).astype(jnp.float32)


def reference(grad_out, grad_side, attn_out, gate_pre, up_pre, seg_ids, down_weight, out_weight):
    onehot = (seg_ids[:, None] == jnp.arange(NSEG, dtype=jnp.int32)[None, :]).astype(jnp.float32)
    counts = jnp.sum(onehot, axis=0)
    length = onehot @ counts
    tok_weight = TOKENS / (NSEG * length)
    grad_scaled = (tok_weight[:, None] * grad_out.astype(jnp.float32)).astype(jnp.bfloat16)
    grad_resid = (grad_scaled.astype(jnp.float32) + grad_side.astype(jnp.float32)).astype(jnp.bfloat16)
    gate_full = gate_pre.astype(jnp.float32)
    up_full = up_pre.astype(jnp.float32)
    sigmoid_gate = jax.nn.sigmoid(gate_full)
    hidden = (gate_full * sigmoid_gate * up_full).astype(jnp.bfloat16)
    col_width = D // N_GZ
    grad_hidden = jnp.zeros((TOKENS, FF), jnp.float32)
    grad_attn = jnp.zeros((TOKENS, HD), jnp.float32)
    for block_id in range(N_GZ):
        lo_col = block_id * col_width
        grad_hidden = grad_hidden + rounded(product_nt(grad_scaled[:, lo_col:lo_col + col_width], down_weight[:, lo_col:lo_col + col_width]))
        grad_attn = grad_attn + rounded(product_nt(grad_resid[:, lo_col:lo_col + col_width], out_weight[:, lo_col:lo_col + col_width]))
    grad_gate = (grad_hidden * up_full * sigmoid_gate * (1.0 + gate_full * (1.0 - sigmoid_gate))).astype(jnp.bfloat16)
    grad_up = (grad_hidden * gate_full * sigmoid_gate).astype(jnp.bfloat16)
    row_width = TOKENS // N_GX
    grad_down = jnp.zeros((FF, D), jnp.float32)
    grad_outproj = jnp.zeros((HD, D), jnp.float32)
    for block_id in range(N_GX):
        lo_row = block_id * row_width
        grad_down = grad_down + rounded(product_tn(hidden[lo_row:lo_row + row_width], grad_scaled[lo_row:lo_row + row_width]))
        grad_outproj = grad_outproj + rounded(product_tn(attn_out[lo_row:lo_row + row_width], grad_resid[lo_row:lo_row + row_width]))
    return grad_gate, grad_up, grad_attn.astype(jnp.bfloat16), grad_down.astype(jnp.bfloat16), grad_outproj.astype(jnp.bfloat16)
```

```python
import jax
import jax.numpy as jnp
from jax import lax
from jax.sharding import PartitionSpec as P

NSEG = 8


def product_nt(lhs_mat, rhs_mat):
    return lax.dot_general(
        lhs_mat, rhs_mat, (((1,), (1,)), ((), ())), preferred_element_type=jnp.float32
    )


def product_tn(lhs_mat, rhs_mat):
    return lax.dot_general(
        lhs_mat, rhs_mat, (((0,), (0,)), ((), ())), preferred_element_type=jnp.float32
    )


def shards(grad_out, grad_side, attn_out, gate_pre, up_pre, seg_ids, down_weight, out_weight):
    row_count = grad_out.shape[0]
    row_start = (lax.axis_index("gx") * lax.axis_size("gy") + lax.axis_index("gy")) * row_count
    onehot = (seg_ids[:, None] == jnp.arange(NSEG, dtype=jnp.int32)[None, :]).astype(jnp.float32)
    counts = jnp.sum(onehot, axis=0)
    own_rows = lax.dynamic_slice_in_dim(onehot, row_start, row_count, 0)
    length = own_rows @ counts
    tok_weight = seg_ids.shape[0] / (NSEG * length)
    grad_scaled = (tok_weight[:, None] * grad_out.astype(jnp.float32)).astype(jnp.bfloat16)
    grad_resid = (grad_scaled.astype(jnp.float32) + grad_side.astype(jnp.float32)).astype(
        jnp.bfloat16
    )
    gate_full = gate_pre.astype(jnp.float32)
    up_full = up_pre.astype(jnp.float32)
    sigmoid_gate = jax.nn.sigmoid(gate_full)
    hidden = (gate_full * sigmoid_gate * up_full).astype(jnp.bfloat16)
    row_blocks = lax.axis_size("gx")

    def columns_in(part):
        rows, cols = part.shape
        spread = part.reshape(rows, row_blocks, cols // row_blocks)
        spread = lax.all_to_all(spread, "gx", split_axis=1, concat_axis=0, tiled=True)
        spread = spread.reshape(row_blocks, rows, cols // row_blocks)
        spread = lax.all_gather(spread, "gz", axis=1, tiled=True)
        return spread.reshape(-1, cols // row_blocks)

    def columns_out(part):
        rows, cols = part.shape
        part = part.astype(jnp.bfloat16).reshape(row_blocks, rows // row_blocks, cols)
        part = lax.psum_scatter(part, "gz", scatter_dimension=1, tiled=True)
        part = lax.all_to_all(part, "gx", split_axis=0, concat_axis=2, tiled=True)
        return part[0].astype(jnp.float32)

    scaled_rows = lax.all_gather(grad_scaled, ("gx", "gy"), axis=0, tiled=True)
    resid_rows = lax.all_gather(grad_resid, ("gx", "gy"), axis=0, tiled=True)
    hidden_rows = columns_in(hidden)
    attn_rows = columns_in(attn_out)
    hidden_part = product_nt(scaled_rows, down_weight)
    attn_part = product_nt(resid_rows, out_weight)
    grad_down = product_tn(hidden_rows, scaled_rows)
    grad_outproj = product_tn(attn_rows, resid_rows)
    grad_hidden = columns_out(hidden_part)
    grad_attn = columns_out(attn_part)
    grad_gate = (
        grad_hidden * up_full * sigmoid_gate * (1.0 + gate_full * (1.0 - sigmoid_gate))
    ).astype(jnp.bfloat16)
    grad_up = (grad_hidden * gate_full * sigmoid_gate).astype(jnp.bfloat16)
    return (
        grad_gate,
        grad_up,
        grad_attn.astype(jnp.bfloat16),
        grad_down.astype(jnp.bfloat16),
        grad_outproj.astype(jnp.bfloat16),
    )


def solution(mesh):
    return jax.shard_map(
        shards,
        mesh=mesh,
        in_specs=(
            P(("gx", "gy"), "gz"),
            P(("gx", "gy"), "gz"),
            P(("gx", "gz"), "gy"),
            P(("gx", "gz"), "gy"),
            P(("gx", "gz"), "gy"),
            P(),
            P(("gy", "gx"), "gz"),
            P(("gy", "gx"), "gz"),
        ),
        out_specs=(
            P(("gx", "gz"), "gy"),
            P(("gx", "gz"), "gy"),
            P(("gx", "gz"), "gy"),
            P(("gy", "gx"), "gz"),
            P(("gy", "gx"), "gz"),
        ),
        check_vma=False,
    )
```

```python
import jax
import jax.numpy as jnp
from jax import lax
from jax.experimental import pallas as pl
from jax.experimental.pallas import tpu as pltpu
from jax.sharding import PartitionSpec as P

NSEG = 8
MESH = pl.DeviceIdType.MESH
F32, BF16 = jnp.float32, jnp.bfloat16

NZ, NX = 8, 4
ROWS = 32
WIDTH = 2048
FF, AT = 832, 256
COLS = AT + FF
TOKENS = 1024
TILE = 256


def product_nt(lhs_mat, rhs_mat):
    return lax.dot_general(lhs_mat, rhs_mat, (((1,), (1,)), ((), ())), preferred_element_type=F32)


def kernel(
    seg_ref, go_ref, gs_ref, attn_ref, gate_ref, up_ref, dw_hbm, ow_hbm,
    ggate_ref, gup_ref, gattn_ref, gdown_hbm, gout_hbm,
    dw, ow, grads, hsend, hid, hid_t, part, xin, yout, yin, dw_out, ow_out,
    w_sem, out_sem, zs, zr, ds, dr, ps, pr, h1s, h1r, h2s, h2r, c1s, c1r, c2s, c2r,
):
    gx, z, gz = lax.axis_index("gx"), lax.axis_index("gy"), lax.axis_index("gz")
    h, c, l, x = gx // 2, gx % 2, gz // NX, gz % NX

    def at(hh, cc, zz, ll, xx):
        return (hh * 2 + cc, zz, ll * NX + xx)

    def send(src, dst, send_sem, recv_sem, device):
        copy = pltpu.make_async_remote_copy(
            src_ref=src, dst_ref=dst, send_sem=send_sem, recv_sem=recv_sem,
            device_id=device, device_id_type=MESH,
        )
        copy.start()

    def sent(ref, sem):
        pltpu.make_async_copy(ref, ref, sem).wait()

    came = sent

    column = [(dh, dc, dl) for dh in range(2) for dc in range(2) for dl in range(2)][1:]

    def in_column(offset):
        dh, dc, dl = offset
        return (h + dh) % 2, (c + dc) % 2, (l + dl) % 2

    right, left = at(h, c, (z + 1) % NZ, l, x), at(h, c, (z + NZ - 1) % NZ, l, x)
    core = at(h, 1 - c, z, l, x)
    across = at(1 - h, c, z, l, x)
    x_right, x_left = at(h, c, z, l, (x + 1) % NX), at(h, c, z, l, (x + NX - 1) % NX)

    copy_dw = pltpu.make_async_copy(dw_hbm, dw, w_sem.at[0])
    copy_ow = pltpu.make_async_copy(ow_hbm, ow, w_sem.at[1])
    copy_dw.start()
    copy_ow.start()

    barrier = pltpu.get_barrier_semaphore()
    peers = [right, left]
    for offset in column:
        hh, cc, ll = in_column(offset)
        peers.append(at(hh, cc, z, ll, x))
    for dx in range(1, NX):
        peers.append(at(h, c, z, l, (x + dx) % NX))
    for peer in peers:
        pl.semaphore_signal(barrier, inc=1, device_id=peer, device_id_type=MESH)

    start = (gx * NZ + z) * ROWS
    seg = jnp.broadcast_to(seg_ref[...], (ROWS, TOKENS))
    token = lax.broadcasted_iota(jnp.int32, (ROWS, TOKENS), 1)
    row = lax.broadcasted_iota(jnp.int32, (ROWS, TOKENS), 0)
    own_id = jnp.sum(jnp.where(token == row + start, seg, 0), axis=1, keepdims=True)
    length = jnp.sum(jnp.where(seg == own_id, 1.0, 0.0).astype(F32), axis=1, keepdims=True)
    tok_weight = TOKENS / (NSEG * length)
    scaled = (tok_weight * go_ref[...].astype(F32)).astype(BF16)
    resid = (scaled.astype(F32) + gs_ref[...].astype(F32)).astype(BF16)
    grads[z, c, h, 0:ROWS] = scaled
    grads[z, c, h, ROWS:2 * ROWS] = resid

    pl.semaphore_wait(barrier, len(peers))

    def block(j, hh, cc=None):
        return grads.at[j, c if cc is None else cc, hh]

    def to_core(j, k, p):
        hh = h if p == 0 else 1 - h
        send(block(j, hh), block(j, hh), ds.at[k, p], dr.at[k, p], core)

    def to_z(direction, s, p, j):
        hh = h if p == 0 else 1 - h
        send(block(j, hh), block(j, hh), zs.at[direction, s, p], zr.at[direction, s, p],
             right if direction == 0 else left)

    send(block(z, h), block(z, h), ps, pr, across)
    to_z(0, 0, 0, z)
    to_z(1, 0, 0, z)
    to_core(z, 0, 0)

    gate = gate_ref[...].astype(F32)
    up = up_ref[...].astype(F32)
    hidden = (gate * jax.nn.sigmoid(gate) * up).astype(BF16)
    for g in range(4):
        hsend[g, :, AT:COLS] = hidden[:, g * FF:(g + 1) * FF]
        hsend[g, :, 0:AT] = attn_ref[:, g * AT:(g + 1) * AT]

    def hid_block(j, cc, hh):
        return hid.at[j, pl.ds(pl.multiple_of((cc * 2 + hh) * ROWS, ROWS), ROWS)]

    for o, offset in enumerate(column):
        hh, cc, ll = in_column(offset)
        send(hsend.at[hh * 2 + cc], hid_block(gz, c, h), h1s.at[o], h1r.at[o], at(hh, cc, z, ll, x))
    hid_block(gz, c, h)[...] = hsend[gx]

    came(block(z, 1 - h), pr)
    to_z(0, 0, 1, z)
    to_z(1, 0, 1, z)
    to_core(z, 0, 1)

    for o, offset in enumerate(column):
        hh, cc, ll = in_column(offset)
        came(hid_block(ll * NX + x, cc, hh), h1r.at[o])

    def chunk(ll, xx):
        return hid.at[ll * NX + xx]

    for i, ll in enumerate((0, 1)):
        send(chunk(ll, x), chunk(ll, x), h2s.at[0, i], h2r.at[0, i], x_right)
    for i, ll in enumerate((1, 0)):
        send(chunk(ll, x), chunk(ll, x), h2s.at[1, i], h2r.at[1, i], x_left)

    copy_dw.wait()
    copy_ow.wait()

    def product(j, k):
        scaled_rows = grads[j, :, :, 0:ROWS].reshape(4 * ROWS, WIDTH)
        resid_rows = grads[j, :, :, ROWS:2 * ROWS].reshape(4 * ROWS, WIDTH)
        part[j, :, AT:COLS] = product_nt(scaled_rows, dw[...]).astype(BF16)
        part[j, :, 0:AT] = product_nt(resid_rows, ow[...]).astype(BF16)
        dx = (j + NX - x) % NX

        @pl.when(dx != 0)
        def _():
            send(part.at[j], xin.at[j // NX, dx - 1], c1s.at[k], c1r.at[j // NX, dx - 1],
                 at(h, c, z, l, j % NX))

    def from_core(j, k, p):
        hh = h if p == 0 else 1 - h
        came(block(j, hh, 1 - c), dr.at[k, p])

    def from_z(direction, s, p, j):
        hh = h if p == 0 else 1 - h
        came(block(j, hh), zr.at[direction, s, p])

    for p in range(2):
        from_core(z, 0, p)
    product(z, 0)

    def relay_hidden():
        came(chunk(0, (x + 3) % NX), h2r.at[0, 0])
        send(chunk(0, (x + 3) % NX), chunk(0, (x + 3) % NX), h2s.at[0, 2], h2r.at[0, 2], x_right)
        came(chunk(1, (x + 1) % NX), h2r.at[1, 0])
        send(chunk(1, (x + 1) % NX), chunk(1, (x + 1) % NX), h2s.at[1, 2], h2r.at[1, 2], x_left)

    def pass_on(s, more):
        for p in range(2):
            for direction in range(2):
                j = (z + NZ - 1 - s) % NZ if direction == 0 else (z + 1 + s) % NZ
                k = 1 + 2 * s + direction
                from_z(direction, s, p, j)
                if more is None:
                    if p == direction:
                        to_z(direction, s + 1, p, j)
                else:
                    to_z(direction, s + 1, p, j)
                to_core(j, k, p)

    def products(s):
        def one(direction, carry):
            j = (z + NZ + (2 * direction - 1) * (1 + s)) % NZ
            k = 1 + 2 * s + direction
            for p in range(2):
                from_core(j, k, p)
            product(j, k)
            return carry

        lax.fori_loop(0, 2, one, 0)

    pass_on(0, True)
    relay_hidden()
    products(0)
    pass_on(1, True)
    products(1)
    pass_on(2, None)
    products(2)
    far = (z + 4) % NZ
    from_z(0, 3, 0, far)
    to_core(far, 7, 0)
    from_z(1, 3, 1, far)
    to_core(far, 7, 1)

    for i, (ll, xx) in enumerate(((0, 3), (1, 3), (0, 2))):
        if i:
            came(chunk(ll, (x + xx) % NX), h2r.at[0, i])
    for i, (ll, xx) in enumerate(((1, 1), (0, 1), (1, 2))):
        if i:
            came(chunk(ll, (x + xx) % NX), h2r.at[1, i])
    for j in range(NZ):
        hid_t[:, j * 4 * ROWS:(j + 1) * 4 * ROWS] = hid[j].T

    for p in range(2):
        from_core(far, 7, p)
    product(far, 7)

    def weight_grads(lo, hi):
        def one(t, carry):
            cols = pl.ds(pl.multiple_of(t * TILE, TILE), TILE)
            scaled_rows = grads[:, :, :, 0:ROWS, cols].reshape(TOKENS, TILE)
            dw_out[:, cols] = jnp.dot(
                hid_t[AT:COLS, :], scaled_rows, preferred_element_type=F32
            ).astype(BF16)
            resid_rows = grads[:, :, :, ROWS:2 * ROWS, cols].reshape(TOKENS, TILE)
            ow_out[:, cols] = jnp.dot(
                hid_t[0:AT, :], resid_rows, preferred_element_type=F32
            ).astype(BF16)
            return carry

        lax.fori_loop(lo, hi, one, 0)

    tiles = WIDTH // TILE
    weight_grads(0, tiles // 2)

    near = jnp.where((x + NZ - z) % NZ <= 2, 0, jnp.where((z + NZ - x) % NZ <= 2, 0, 1))

    def sum_x(ll, o_first):
        for dx in range(3):
            came(xin.at[ll, dx], c1r.at[ll, dx])
        total = part[ll * NX + x].astype(F32)
        for dx in range(3):
            total = total + xin[ll, dx].astype(F32)
        yout[ll] = total.astype(BF16)

    def yout_block(ll, cc, hh):
        return yout.at[ll, pl.ds(pl.multiple_of((cc * 2 + hh) * ROWS, ROWS), ROWS)]

    def send_y(dl):
        ll = (l + dl) % 2
        for o, offset in enumerate(column):
            if offset[2] == dl:
                hh, cc, _ = in_column(offset)
                send(yout_block(ll, cc, hh), yin.at[gx, l], c2s.at[o], c2r.at[o], at(hh, cc, z, ll, x))
        if dl == 0:
            yin[gx, l] = yout_block(l, c, h)[...]

    for dl in range(2):
        sum_x((l + dl) % 2, dl)
        send_y(dl)

    weight_grads(tiles // 2, tiles)
    copy_gd = pltpu.make_async_copy(dw_out, gdown_hbm, out_sem.at[0])
    copy_go = pltpu.make_async_copy(ow_out, gout_hbm, out_sem.at[1])
    copy_gd.start()
    copy_go.start()

    for o, offset in enumerate(column):
        hh, cc, ll = in_column(offset)
        came(yin.at[hh * 2 + cc, ll], c2r.at[o])
    summed = []
    for g in range(4):
        total = yin[g, 0].astype(F32) + yin[g, 1].astype(F32)
        gattn_ref[:, g * AT:(g + 1) * AT] = total[:, 0:AT].astype(BF16)
        summed.append(total[:, AT:COLS])
    grad_hidden = jnp.concatenate(summed, axis=1)
    gate = gate_ref[...].astype(F32)
    up = up_ref[...].astype(F32)
    sig = jax.nn.sigmoid(gate)
    ggate_ref[...] = (grad_hidden * up * sig * (1.0 + gate * (1.0 - sig))).astype(BF16)
    gup_ref[...] = (grad_hidden * gate * sig).astype(BF16)

    own = block(z, h)
    sent(own, ps)
    for s in range(4):
        for p in range(2):
            for direction in range(2):
                if s < 3 or p == direction:
                    sent(own, zs.at[direction, s, p])
    for k in range(8):
        for p in range(2):
            sent(own, ds.at[k, p])
    for o in range(7):
        sent(hsend.at[0], h1s.at[o])
        sent(yin.at[0, 0], c2s.at[o])
    for direction in range(2):
        for i in range(3):
            sent(hid.at[0], h2s.at[direction, i])
    for k in range(8):
        j = (z if k == 0 else (z + 4 if k == 7 else (z + NZ + (2 * ((k - 1) % 2) - 1) * (1 + (k - 1) // 2)))) % NZ

        @pl.when((j + NX - x) % NX != 0)
        def _():
            sent(part.at[0], c1s.at[k])

    copy_gd.wait()
    copy_go.wait()


def shards(grad_out, grad_side, attn_out, gate_pre, up_pre, seg_ids, down_weight, out_weight):
    vmem = pl.BlockSpec(memory_space=pltpu.VMEM)
    hbm = pl.BlockSpec(memory_space=pl.ANY)
    dma = pltpu.SemaphoreType.DMA
    return pl.pallas_call(
        kernel,
        out_shape=(
            jax.ShapeDtypeStruct(gate_pre.shape, BF16),
            jax.ShapeDtypeStruct(up_pre.shape, BF16),
            jax.ShapeDtypeStruct(attn_out.shape, BF16),
            jax.ShapeDtypeStruct(down_weight.shape, BF16),
            jax.ShapeDtypeStruct(out_weight.shape, BF16),
        ),
        in_specs=[vmem] * 6 + [hbm] * 2,
        out_specs=(vmem, vmem, vmem, hbm, hbm),
        scratch_shapes=[
            pltpu.VMEM((FF, WIDTH), BF16),
            pltpu.VMEM((AT, WIDTH), BF16),
            pltpu.VMEM((NZ, 2, 2, 2 * ROWS, WIDTH), BF16),
            pltpu.VMEM((4, ROWS, COLS), BF16),
            pltpu.VMEM((NZ, 4 * ROWS, COLS), BF16),
            pltpu.VMEM((COLS, TOKENS), BF16),
            pltpu.VMEM((NZ, 4 * ROWS, COLS), BF16),
            pltpu.VMEM((2, 3, 4 * ROWS, COLS), BF16),
            pltpu.VMEM((2, 4 * ROWS, COLS), BF16),
            pltpu.VMEM((4, 2, ROWS, COLS), BF16),
            pltpu.VMEM((FF, WIDTH), BF16),
            pltpu.VMEM((AT, WIDTH), BF16),
            dma((2,)),
            dma((2,)),
            dma((2, 4, 2)),
            dma((2, 4, 2)),
            dma((8, 2)),
            dma((8, 2)),
            dma,
            dma,
            dma((7,)),
            dma((7,)),
            dma((2, 3)),
            dma((2, 3)),
            dma((8,)),
            dma((2, 3)),
            dma((7,)),
            dma((7,)),
        ],
        compiler_params=pltpu.CompilerParams(
            collective_id=0, has_side_effects=True, vmem_limit_bytes=56 * 2**20
        ),
        cost_estimate=pl.CostEstimate(
            flops=4 * TOKENS * WIDTH * COLS, bytes_accessed=20 * 2**20, transcendentals=0
        ),
    )(
        seg_ids.reshape(1, TOKENS), grad_out, grad_side, attn_out, gate_pre, up_pre,
        down_weight, out_weight,
    )


def solution(mesh):
    return jax.shard_map(
        shards,
        mesh=mesh,
        in_specs=(
            P(("gx", "gy"), "gz"),
            P(("gx", "gy"), "gz"),
            P(("gx", "gz"), "gy"),
            P(("gx", "gz"), "gy"),
            P(("gx", "gz"), "gy"),
            P(),
            P(("gy", "gx"), "gz"),
            P(("gy", "gx"), "gz"),
        ),
        out_specs=(
            P(("gx", "gz"), "gy"),
            P(("gx", "gz"), "gy"),
            P(("gx", "gz"), "gy"),
            P(("gy", "gx"), "gz"),
            P(("gy", "gx"), "gz"),
        ),
        check_vma=False,
    )
```

```python
import jax
import jax.numpy as jnp
from jax import lax
from jax.experimental import pallas as pl
from jax.experimental.pallas import tpu as pltpu
from jax.sharding import PartitionSpec as P

NSEG = 8
MESH = pl.DeviceIdType.MESH
F32, BF16 = jnp.float32, jnp.bfloat16

NZ, NX = 8, 4
ROWS = 32
WIDTH = 2048
FF, AT = 832, 256
COLS = AT + FF
TOKENS = 1024
TILE = 256


def product_nt(lhs_mat, rhs_mat):
    return lax.dot_general(lhs_mat, rhs_mat, (((1,), (1,)), ((), ())), preferred_element_type=F32)


def kernel(
    seg_ref, go_ref, gs_ref, attn_ref, gate_ref, up_ref, dw_hbm, ow_hbm,
    ggate_ref, gup_ref, gattn_ref, dw_out, ow_out,
    dw, ow, grads, hsend, hx, hid, hid_t, part_f, part_a, xin_f, xin_a, yout_f, yout_a, yin_f, yin_a,
    w_sem, zs, zr, ds, dr, ps, pr, h1s, h1r, h2s, h2r, c1s, c1r, c2s, c2r,
):
    gx, z, gz = lax.axis_index("gx"), lax.axis_index("gy"), lax.axis_index("gz")
    h, c, l, x = gx // 2, gx % 2, gz // NX, gz % NX
    weights, part, xin = (dw, ow), (part_f, part_a), (xin_f, xin_a)
    yout, yin = (yout_f, yout_a), (yin_f, yin_a)

    def at(hh, cc, zz, ll, xx):
        return (hh * 2 + cc, zz, ll * NX + xx)

    def send(src, dst, send_sem, recv_sem, device):
        copy = pltpu.make_async_remote_copy(
            src_ref=src, dst_ref=dst, send_sem=send_sem, recv_sem=recv_sem,
            device_id=device, device_id_type=MESH,
        )
        copy.start()

    def sent(ref, sem):
        pltpu.make_async_copy(ref, ref, sem).wait()

    came = sent

    column = [(dh, dc, dl) for dh in range(2) for dc in range(2) for dl in range(2)][1:]

    def in_column(offset):
        dh, dc, dl = offset
        return (h + dh) % 2, (c + dc) % 2, (l + dl) % 2

    right, left = at(h, c, (z + 1) % NZ, l, x), at(h, c, (z + NZ - 1) % NZ, l, x)
    core = at(h, 1 - c, z, l, x)
    across = at(1 - h, c, z, l, x)

    copy_dw = pltpu.make_async_copy(dw_hbm, dw, w_sem.at[0])
    copy_ow = pltpu.make_async_copy(ow_hbm, ow, w_sem.at[1])
    copy_dw.start()
    copy_ow.start()

    barrier = pltpu.get_barrier_semaphore()
    peers = [right, left]
    for offset in column:
        hh, cc, ll = in_column(offset)
        peers.append(at(hh, cc, z, ll, x))
    for dx in range(1, NX):
        peers.append(at(h, c, z, l, (x + dx) % NX))
    for peer in peers:
        pl.semaphore_signal(barrier, inc=1, device_id=peer, device_id_type=MESH)

    def rows_of(ref, cc, hh):
        return ref.at[pl.ds(pl.multiple_of((cc * 2 + hh) * ROWS, ROWS), ROWS)]

    def block(q, j, hh, cc=None):
        return rows_of(grads.at[q, j], c if cc is None else cc, hh)

    start = (gx * NZ + z) * ROWS
    seg = jnp.broadcast_to(seg_ref[...], (ROWS, TOKENS))
    token = lax.broadcasted_iota(jnp.int32, (ROWS, TOKENS), 1)
    row = lax.broadcasted_iota(jnp.int32, (ROWS, TOKENS), 0)
    own_id = jnp.sum(jnp.where(token == row + start, seg, 0), axis=1, keepdims=True)
    length = jnp.sum(jnp.where(seg == own_id, 1.0, 0.0).astype(F32), axis=1, keepdims=True)
    tok_weight = TOKENS / (NSEG * length)
    scaled = (tok_weight * go_ref[...].astype(F32)).astype(BF16)
    block(0, z, h)[...] = scaled
    block(1, z, h)[...] = (scaled.astype(F32) + gs_ref[...].astype(F32)).astype(BF16)

    def to_core(q, j, k, p):
        hh = h if p == 0 else 1 - h
        send(block(q, j, hh), block(q, j, hh), ds.at[q, k, p], dr.at[q, k, p], core)

    def to_z(q, direction, s, p, j):
        hh = h if p == 0 else 1 - h
        send(block(q, j, hh), block(q, j, hh), zs.at[q, direction, s, p], zr.at[q, direction, s, p],
             right if direction == 0 else left)

    def from_core(q, j, k, p):
        hh = h if p == 0 else 1 - h
        came(block(q, j, hh, 1 - c), dr.at[q, k, p])

    def from_z(q, direction, s, p, j):
        hh = h if p == 0 else 1 - h
        came(block(q, j, hh), zr.at[q, direction, s, p])

    gate = gate_ref[...].astype(F32)
    up = up_ref[...].astype(F32)
    hidden = (gate * jax.nn.sigmoid(gate) * up).astype(BF16)
    for g in range(4):
        hsend[g, :, AT:COLS] = hidden[:, g * FF:(g + 1) * FF]
        hsend[g, :, 0:AT] = attn_ref[:, g * AT:(g + 1) * AT]

    pl.semaphore_wait(barrier, len(peers))

    def hid_block(ll, xx, cc, hh):
        return rows_of(hid.at[ll * NX + xx], cc, hh)

    def hidden_along_x():
        for dx in (1, 3, 2):
            send(hsend, hx.at[dx - 1], h1s.at[dx - 1], h1r.at[dx - 1], at(h, c, z, l, (x + NX - dx) % NX))

    def hidden_along_y(dx):
        source = hsend
        if dx:
            source = hx.at[dx - 1]
            came(source, h1r.at[dx - 1])
        xx = (x + dx) % NX
        for o, offset in enumerate(column):
            hh, cc, ll = in_column(offset)
            send(source.at[hh * 2 + cc], hid_block(l, xx, c, h), h2s.at[dx, o], h2r.at[dx, o],
                 at(hh, cc, z, ll, x))
        hid_block(l, xx, c, h)[...] = source[gx]

    def rest_of_hidden():
        for dx in range(NX):
            for o, offset in enumerate(column):
                hh, cc, ll = in_column(offset)
                came(hid_block(ll, (x + dx) % NX, cc, hh), h2r.at[dx, o])
        for j in range(NZ):
            hid_t[:, j * 4 * ROWS:(j + 1) * 4 * ROWS] = hid[j].T

    send(block(0, z, h), block(0, z, h), ps.at[0], pr.at[0], across)
    to_z(0, 0, 0, 0, z)
    to_z(0, 1, 0, 0, z)
    to_core(0, z, 0, 0)
    hidden_along_x()
    to_z(1, 0, 0, 0, z)
    to_z(1, 1, 0, 0, z)
    came(block(0, z, 1 - h), pr.at[0])
    to_z(0, 0, 0, 1, z)
    to_z(0, 1, 0, 1, z)
    to_core(0, z, 0, 1)
    send(block(1, z, h), block(1, z, h), ps.at[1], pr.at[1], across)
    hidden_along_y(0)

    def product(q, j, k):
        for p in range(2):
            from_core(q, j, k, p)
        part[q][j] = product_nt(grads[q, j], weights[q][...]).astype(BF16)
        dx = (j + NX - x) % NX

        @pl.when(dx != 0)
        def _():
            send(part[q].at[j], xin[q].at[j // NX, dx - 1], c1s.at[q, k], c1r.at[q, j // NX, dx - 1],
                 at(h, c, z, l, j % NX))

    def pass_on(q, s):
        for p in range(2):
            for direction in range(2):
                j = (z + NZ - 1 - s) % NZ if direction == 0 else (z + 1 + s) % NZ
                from_z(q, direction, s, p, j)
                if s < 2 or p == direction:
                    to_z(q, direction, s + 1, p, j)
                to_core(q, j, 1 + 2 * s + direction, p)

    def products(q, s):
        def one(direction, carry):
            product(q, (z + NZ + (2 * direction - 1) * (1 + s)) % NZ, 1 + 2 * s + direction)
            return carry

        lax.fori_loop(0, 2, one, 0)

    far = (z + 4) % NZ

    def pass_far(q):
        for p in range(2):
            from_z(q, p, 3, p, far)
            to_core(q, far, 7, p)

    def weight_grad(q, lo, hi):
        lhs, out = ((hid_t.at[AT:COLS], dw_out), (hid_t.at[0:AT], ow_out))[q]

        def one(t, carry):
            cols = pl.ds(pl.multiple_of(t * TILE, TILE), TILE)
            rows = grads[q, :, :, cols].reshape(TOKENS, TILE)
            out[:, cols] = jnp.dot(lhs[...], rows, preferred_element_type=F32).astype(BF16)
            return carry

        lax.fori_loop(lo, hi, one, 0)

    def sum_x(q, ll):
        for dx in range(3):
            came(xin[q].at[ll, dx], c1r.at[q, ll, dx])
        total = part[q][ll * NX + x].astype(F32)
        for dx in range(3):
            total = total + xin[q][ll, dx].astype(F32)
        yout[q][ll] = total.astype(BF16)

    def send_y(q, dl):
        ll = (l + dl) % 2
        for o, offset in enumerate(column):
            if offset[2] == dl:
                hh, cc, _ = in_column(offset)
                send(rows_of(yout[q].at[ll], cc, hh), yin[q].at[gx, l], c2s.at[q, o], c2r.at[q, o],
                     at(hh, cc, z, ll, x))
        if dl == 0:
            yin[q][gx, l] = rows_of(yout[q].at[l], c, h)[...]

    def summed(q):
        for o, offset in enumerate(column):
            hh, cc, ll = in_column(offset)
            came(yin[q].at[hh * 2 + cc, ll], c2r.at[q, o])
        return [yin[q][g, 0].astype(F32) + yin[q][g, 1].astype(F32) for g in range(4)]

    pass_on(0, 0)
    copy_dw.wait()
    copy_ow.wait()
    product(0, z, 0)
    pass_on(0, 1)
    hidden_along_y(1)
    hidden_along_y(3)
    products(0, 0)
    pass_on(0, 2)
    came(block(1, z, 1 - h), pr.at[1])
    to_z(1, 0, 0, 1, z)
    to_z(1, 1, 0, 1, z)
    to_core(1, z, 0, 0)
    to_core(1, z, 0, 1)
    hidden_along_y(2)
    products(0, 1)
    pass_far(0)
    products(0, 2)
    pass_on(1, 0)
    product(0, far, 7)
    product(1, z, 0)
    products(1, 0)
    pass_on(1, 1)
    rest_of_hidden()
    products(1, 1)
    weight_grad(0, 0, 3)
    pass_on(1, 2)
    products(1, 2)
    for dl in range(2):
        sum_x(0, (l + dl) % 2)
        send_y(0, dl)
    weight_grad(0, 3, 5)
    pass_far(1)
    product(1, far, 7)
    weight_grad(0, 5, 8)
    weight_grad(1, 0, 8)
    for dl in range(2):
        sum_x(1, (l + dl) % 2)
        send_y(1, dl)

    grad_hidden = jnp.concatenate(summed(0), axis=1)
    gate = gate_ref[...].astype(F32)
    up = up_ref[...].astype(F32)
    sig = jax.nn.sigmoid(gate)
    ggate_ref[...] = (grad_hidden * up * sig * (1.0 + gate * (1.0 - sig))).astype(BF16)
    gup_ref[...] = (grad_hidden * gate * sig).astype(BF16)
    gattn_ref[...] = jnp.concatenate(summed(1), axis=1).astype(BF16)

    own = block(0, z, h)
    for q in range(2):
        sent(own, ps.at[q])
        for s in range(4):
            for p in range(2):
                for direction in range(2):
                    if s < 3 or p == direction:
                        sent(own, zs.at[q, direction, s, p])
        for k in range(8):
            for p in range(2):
                sent(own, ds.at[q, k, p])
        for o in range(7):
            sent(yin[q].at[0, 0], c2s.at[q, o])
        for k in range(8):
            step, sign = (k + 1) // 2, 2 * ((k + 1) % 2) - 1
            j = (z + NZ + (sign * step if k else 0)) % NZ

            @pl.when((j + NX - x) % NX != 0)
            def _():
                sent(part[q].at[0], c1s.at[q, k])

    for dx in range(3):
        sent(hsend, h1s.at[dx])
    for dx in range(NX):
        for o in range(7):
            sent(hsend.at[0], h2s.at[dx, o])


PIECES = (1, 1, 1, 4, 2)


def copy_out(*refs):
    sources, results, sem = refs[:5], refs[5:10], refs[10]
    copies = []
    for source, result, pieces in zip(sources, results, PIECES):
        rows = source.shape[0] // pieces
        for i in range(pieces):
            part = pl.ds(i * rows, rows)
            copies.append(pltpu.make_async_copy(source.at[part], result.at[part], sem.at[len(copies)]))
    for copy in copies:
        copy.start()
    for copy in copies:
        copy.wait()


def shards(grad_out, grad_side, attn_out, gate_pre, up_pre, seg_ids, down_weight, out_weight):
    vmem = pl.BlockSpec(memory_space=pltpu.VMEM)
    hbm = pl.BlockSpec(memory_space=pl.ANY)
    dma = pltpu.SemaphoreType.DMA
    shapes = tuple(
        jax.ShapeDtypeStruct(like.shape, BF16)
        for like in (gate_pre, up_pre, attn_out, down_weight, out_weight)
    )
    results = pl.pallas_call(
        kernel,
        out_shape=tuple(pltpu.VMEM(like.shape, BF16) for like in shapes),
        in_specs=[vmem] * 6 + [pl.BlockSpec(memory_space=pltpu.HBM)] * 2,
        out_specs=(vmem,) * 5,
        scratch_shapes=[
            pltpu.VMEM((FF, WIDTH), BF16),
            pltpu.VMEM((AT, WIDTH), BF16),
            pltpu.VMEM((2, NZ, 4 * ROWS, WIDTH), BF16),
            pltpu.VMEM((4, ROWS, COLS), BF16),
            pltpu.VMEM((3, 4, ROWS, COLS), BF16),
            pltpu.VMEM((NZ, 4 * ROWS, COLS), BF16),
            pltpu.VMEM((COLS, TOKENS), BF16),
            pltpu.VMEM((NZ, 4 * ROWS, FF), BF16),
            pltpu.VMEM((NZ, 4 * ROWS, AT), BF16),
            pltpu.VMEM((2, 3, 4 * ROWS, FF), BF16),
            pltpu.VMEM((2, 3, 4 * ROWS, AT), BF16),
            pltpu.VMEM((2, 4 * ROWS, FF), BF16),
            pltpu.VMEM((2, 4 * ROWS, AT), BF16),
            pltpu.VMEM((4, 2, ROWS, FF), BF16),
            pltpu.VMEM((4, 2, ROWS, AT), BF16),
            dma((2,)),
            dma((2, 2, 4, 2)),
            dma((2, 2, 4, 2)),
            dma((2, 8, 2)),
            dma((2, 8, 2)),
            dma((2,)),
            dma((2,)),
            dma((3,)),
            dma((3,)),
            dma((4, 7)),
            dma((4, 7)),
            dma((2, 8)),
            dma((2, 2, 3)),
            dma((2, 7)),
            dma((2, 7)),
        ],
        compiler_params=pltpu.CompilerParams(
            collective_id=0, has_side_effects=True, vmem_limit_bytes=56 * 2**20
        ),
        cost_estimate=pl.CostEstimate(
            flops=4 * TOKENS * WIDTH * COLS, bytes_accessed=20 * 2**20, transcendentals=0
        ),
    )(
        seg_ids.reshape(1, TOKENS), grad_out, grad_side, attn_out, gate_pre, up_pre,
        down_weight, out_weight,
    )
    return pl.pallas_call(
        copy_out,
        out_shape=shapes,
        in_specs=[vmem] * 5,
        out_specs=(hbm,) * 5,
        scratch_shapes=[dma((sum(PIECES),))],
        compiler_params=pltpu.CompilerParams(vmem_limit_bytes=20 * 2**20),
    )(*results)


def solution(mesh):
    return jax.shard_map(
        shards,
        mesh=mesh,
        in_specs=(
            P(("gx", "gy"), "gz"),
            P(("gx", "gy"), "gz"),
            P(("gx", "gz"), "gy"),
            P(("gx", "gz"), "gy"),
            P(("gx", "gz"), "gy"),
            P(),
            P(("gy", "gx"), "gz"),
            P(("gy", "gx"), "gz"),
        ),
        out_specs=(
            P(("gx", "gz"), "gy"),
            P(("gx", "gz"), "gy"),
            P(("gx", "gz"), "gy"),
            P(("gy", "gx"), "gz"),
            P(("gy", "gx"), "gz"),
        ),
        check_vma=False,
    )
```

```python
import jax
import jax.numpy as jnp
from jax import lax
from jax.experimental import pallas as pl
from jax.experimental.pallas import tpu as pltpu
from jax.sharding import PartitionSpec as P

NSEG = 8
MESH = pl.DeviceIdType.MESH
F32, BF16 = jnp.float32, jnp.bfloat16

NZ, NX = 8, 4
ROWS = 32
WIDTH = 2048
FF, AT = 832, 256
COLS = AT + FF
TOKENS = 1024
TILE = 256


def product_nt(lhs_mat, rhs_mat):
    return lax.dot_general(lhs_mat, rhs_mat, (((1,), (1,)), ((), ())), preferred_element_type=F32)


def kernel(
    seg_hbm, go_hbm, gs_hbm, attn_hbm, gate_hbm, up_hbm, dw_hbm, ow_hbm,
    ggate_ref, gup_ref, gattn_ref, dw_out, ow_out,
    seg_ref, go_ref, gs_ref, attn_ref, gate_ref, up_ref, dw, ow, grads, hsend, hx, hid, hid_t, part_f, part_a, xin_f, xin_a, yout_f, yout_a, yin_f, yin_a,
    w_sem, zs, zr, ds, dr, ps, pr, h1s, h1r, h2s, h2r, c1s, c1r, c2s, c2r,
):
    gx, z, gz = lax.axis_index("gx"), lax.axis_index("gy"), lax.axis_index("gz")
    h, c, l, x = gx // 2, gx % 2, gz // NX, gz % NX
    weights, part, xin = (dw, ow), (part_f, part_a), (xin_f, xin_a)
    yout, yin = (yout_f, yout_a), (yin_f, yin_a)

    def at(hh, cc, zz, ll, xx):
        return (hh * 2 + cc, zz, ll * NX + xx)

    def send(src, dst, send_sem, recv_sem, device):
        copy = pltpu.make_async_remote_copy(
            src_ref=src, dst_ref=dst, send_sem=send_sem, recv_sem=recv_sem,
            device_id=device, device_id_type=MESH,
        )
        copy.start()

    def sent(ref, sem):
        pltpu.make_async_copy(ref, ref, sem).wait()

    came = sent

    column = [(dh, dc, dl) for dh in range(2) for dc in range(2) for dl in range(2)][1:]

    def in_column(offset):
        dh, dc, dl = offset
        return (h + dh) % 2, (c + dc) % 2, (l + dl) % 2

    right, left = at(h, c, (z + 1) % NZ, l, x), at(h, c, (z + NZ - 1) % NZ, l, x)
    core = at(h, 1 - c, z, l, x)
    across = at(1 - h, c, z, l, x)

    barrier = pltpu.get_barrier_semaphore()
    peers = [right, left]
    for offset in column:
        hh, cc, ll = in_column(offset)
        peers.append(at(hh, cc, z, ll, x))
    for dx in range(1, NX):
        peers.append(at(h, c, z, l, (x + dx) % NX))
    for peer in peers:
        pl.semaphore_signal(barrier, inc=1, device_id=peer, device_id_type=MESH)

    fetches = [
        pltpu.make_async_copy(source, target, w_sem.at[i])
        for i, (source, target) in enumerate((
            (seg_hbm, seg_ref), (go_hbm, go_ref), (gs_hbm, gs_ref), (gate_hbm, gate_ref),
            (up_hbm, up_ref), (attn_hbm, attn_ref), (dw_hbm, dw), (ow_hbm, ow),
        ))
    ]
    for fetch in fetches:
        fetch.start()

    def rows_of(ref, cc, hh):
        return ref.at[pl.ds(pl.multiple_of((cc * 2 + hh) * ROWS, ROWS), ROWS)]

    def block(q, j, hh, cc=None):
        return rows_of(grads.at[q, j], c if cc is None else cc, hh)

    for fetch in fetches[:3]:
        fetch.wait()
    start = (gx * NZ + z) * ROWS
    seg = jnp.broadcast_to(seg_ref[...], (ROWS, TOKENS))
    token = lax.broadcasted_iota(jnp.int32, (ROWS, TOKENS), 1)
    row = lax.broadcasted_iota(jnp.int32, (ROWS, TOKENS), 0)
    own_id = jnp.sum(jnp.where(token == row + start, seg, 0), axis=1, keepdims=True)
    length = jnp.sum(jnp.where(seg == own_id, 1.0, 0.0).astype(F32), axis=1, keepdims=True)
    tok_weight = TOKENS / (NSEG * length)
    scaled = (tok_weight * go_ref[...].astype(F32)).astype(BF16)
    block(0, z, h)[...] = scaled
    block(1, z, h)[...] = (scaled.astype(F32) + gs_ref[...].astype(F32)).astype(BF16)

    def to_core(q, j, k, p):
        hh = h if p == 0 else 1 - h
        send(block(q, j, hh), block(q, j, hh), ds, dr.at[q, k], core)

    def to_z(q, direction, s, p, j):
        hh = h if p == 0 else 1 - h
        send(block(q, j, hh), block(q, j, hh), zs, zr.at[q, direction, s, p],
             right if direction == 0 else left)

    def from_core(q, j, k):
        came(grads.at[q, j, 0:2 * ROWS], dr.at[q, k])

    def from_z(q, direction, s, p, j):
        hh = h if p == 0 else 1 - h
        came(block(q, j, hh), zr.at[q, direction, s, p])

    pl.semaphore_wait(barrier, len(peers))

    def hid_block(ll, xx, cc, hh):
        return rows_of(hid.at[ll * NX + xx], cc, hh)

    def hidden_along_x():
        for dx in (1, 3, 2):
            send(hsend, hx.at[dx - 1], h1s, h1r.at[dx - 1], at(h, c, z, l, (x + NX - dx) % NX))

    def hidden_along_y(dx):
        source = hsend
        if dx:
            source = hx.at[dx - 1]
            came(source, h1r.at[dx - 1])
        xx = (x + dx) % NX
        for offset in column:
            if offset[0] <= offset[2]:
                hh, cc, ll = in_column(offset)
                send(source.at[hh * 2 + cc], hid_block(l, xx, c, h), h2s, h2r.at[dx, offset[0]],
                     at(hh, cc, z, ll, x))
        hid_block(l, xx, c, h)[...] = source[gx]

    def relay_hidden(dx):
        came(hid.at[0:2, 0:ROWS], h2r.at[dx, 1])
        for cc in range(2):
            rows = hid_block(1 - l, (x + dx) % NX, cc, 1 - h)
            send(rows, rows, h2s, h2r.at[dx, 0], at(h, c, z, 1 - l, x))

    def turn_hidden(dx):
        came(hid.at[0:5, 0:ROWS], h2r.at[dx, 0])
        for ll in range(2):
            j = ll * NX + (x + dx) % NX
            hid_t[:, pl.ds(pl.multiple_of(j * 4 * ROWS, 4 * ROWS), 4 * ROWS)] = hid[j].T

    send(block(0, z, h), block(0, z, h), ps, pr.at[0], across)
    to_z(0, 0, 0, 0, z)
    to_z(0, 1, 0, 0, z)
    to_core(0, z, 0, 0)
    for fetch in fetches[3:6]:
        fetch.wait()
    gate = gate_ref[...].astype(F32)
    up = up_ref[...].astype(F32)
    hidden = (gate * jax.nn.sigmoid(gate) * up).astype(BF16)
    for g in range(4):
        hsend[g, :, AT:COLS] = hidden[:, g * FF:(g + 1) * FF]
        hsend[g, :, 0:AT] = attn_ref[:, g * AT:(g + 1) * AT]
    hidden_along_x()
    to_z(1, 0, 0, 0, z)
    to_z(1, 1, 0, 0, z)
    came(block(0, z, 1 - h), pr.at[0])
    to_z(0, 0, 0, 1, z)
    to_z(0, 1, 0, 1, z)
    to_core(0, z, 0, 1)
    send(block(1, z, h), block(1, z, h), ps, pr.at[1], across)
    hidden_along_y(0)

    def product(q, j, k):
        from_core(q, j, k)
        part[q][j] = product_nt(grads[q, j], weights[q][...]).astype(BF16)
        dx = (j + NX - x) % NX

        @pl.when(dx != 0)
        def _():
            send(part[q].at[j], xin[q].at[j // NX, dx - 1], c1s.at[q], c1r.at[q, j // NX],
                 at(h, c, z, l, j % NX))

    def beyond(direction, s):
        return (z + NZ - 1 - s) % NZ if direction == 0 else (z + 1 + s) % NZ

    def cross_resid():
        for direction in range(2):
            j = beyond(direction, 0)
            from_z(1, direction, 0, 0, j)
            send(block(1, j, h), block(1, j, h), ps, pr.at[2 + direction], across)
            to_core(1, j, 1 + direction, 0)

    def pass_half(q, s, p):
        for direction in range(2):
            j = beyond(direction, s)
            crossed = q == 1 and s == 0
            if crossed and p == 1:
                came(block(1, j, 1 - h), pr.at[2 + direction])
            elif not crossed:
                from_z(q, direction, s, p, j)
            if s < 2 or p == direction:
                to_z(q, direction, s + 1, p, j)
            if not crossed or p == 1:
                to_core(q, j, 1 + 2 * s + direction, p)

    def pass_on(q, s):
        for p in range(2):
            pass_half(q, s, p)

    def products(q, s):
        def one(direction, carry):
            product(q, (z + NZ + (2 * direction - 1) * (1 + s)) % NZ, 1 + 2 * s + direction)
            return carry

        lax.fori_loop(0, 2, one, 0)

    far = (z + 4) % NZ

    def pass_far(q):
        for p in range(2):
            from_z(q, p, 3, p, far)
            to_core(q, far, 7, p)

    def weight_grad(q, lo, hi):
        lhs, out = ((hid_t.at[AT:COLS], dw_out), (hid_t.at[0:AT], ow_out))[q]

        def one(t, carry):
            cols = pl.ds(pl.multiple_of(t * TILE, TILE), TILE)
            rows = grads[q, :, :, cols].reshape(TOKENS, TILE)
            out[:, cols] = jnp.dot(lhs[...], rows, preferred_element_type=F32).astype(BF16)
            return carry

        lax.fori_loop(lo, hi, one, 0)

    def sum_x(q, ll):
        came(xin[q].at[ll], c1r.at[q, ll])
        total = part[q][ll * NX + x].astype(F32)
        for dx in range(3):
            total = total + xin[q][ll, dx].astype(F32)
        yout[q][ll] = total.astype(BF16)

    def send_y(q, dl):
        ll = (l + dl) % 2
        for o, offset in enumerate(column):
            if offset[2] == dl:
                hh, cc, _ = in_column(offset)
                send(rows_of(yout[q].at[ll], cc, hh), yin[q].at[gx * 2 + l], c2s.at[q], c2r.at[q],
                     at(hh, cc, z, ll, x))
        if dl == 0:
            yin[q][gx * 2 + l] = rows_of(yout[q].at[l], c, h)[...]

    def summed(q):
        came(yin[q].at[0:7], c2r.at[q])
        return [yin[q][2 * g].astype(F32) + yin[q][2 * g + 1].astype(F32) for g in range(4)]

    pass_on(0, 0)
    for fetch in fetches[6:]:
        fetch.wait()
    cross_resid()
    product(0, z, 0)
    pass_on(0, 1)
    relay_hidden(0)
    hidden_along_y(1)
    hidden_along_y(3)
    products(0, 0)
    pass_on(0, 2)
    came(block(1, z, 1 - h), pr.at[1])
    to_core(1, z, 0, 0)
    to_core(1, z, 0, 1)
    pass_on(1, 0)
    hidden_along_y(2)
    products(0, 1)
    pass_far(0)
    products(0, 2)
    relay_hidden(1)
    relay_hidden(3)
    product(0, far, 7)
    product(1, z, 0)
    products(1, 0)
    pass_on(1, 1)
    products(1, 1)
    relay_hidden(2)
    pass_half(1, 2, 0)
    turn_hidden(0)
    turn_hidden(1)
    pass_half(1, 2, 1)
    products(1, 2)
    turn_hidden(3)
    turn_hidden(2)
    for dl in range(2):
        sum_x(0, (l + dl) % 2)
        send_y(0, dl)
    weight_grad(0, 0, 2)
    pass_far(1)
    product(1, far, 7)
    weight_grad(0, 2, 7)
    for dl in range(2):
        sum_x(1, (l + dl) % 2)
        send_y(1, dl)
    weight_grad(0, 7, 8)
    weight_grad(1, 0, 8)

    grad_hidden = jnp.concatenate(summed(0), axis=1)
    gate = gate_ref[...].astype(F32)
    up = up_ref[...].astype(F32)
    sig = jax.nn.sigmoid(gate)
    ggate_ref[...] = (grad_hidden * up * sig * (1.0 + gate * (1.0 - sig))).astype(BF16)
    gup_ref[...] = (grad_hidden * gate * sig).astype(BF16)
    gattn_ref[...] = jnp.concatenate(summed(1), axis=1).astype(BF16)

    sent(grads.at[0, 0], ps)
    sent(grads.at[0, 0:6], zs)
    sent(grads.at[0, 0, 0:2 * ROWS], zs)
    sent(grads.at[0], ds)
    sent(hx, h1s)
    sent(hid.at[0:7], h2s)
    for q in range(2):
        sent(part[q].at[0:6], c1s.at[q])
        sent(yin[q].at[0:7], c2s.at[q])


PIECES = (1, 1, 1, 4, 2)


def copy_out(*refs):
    sources, results, sem = refs[:5], refs[5:10], refs[10]
    copies = []
    for source, result, pieces in zip(sources, results, PIECES):
        rows = source.shape[0] // pieces
        for i in range(pieces):
            part = pl.ds(i * rows, rows)
            copies.append(pltpu.make_async_copy(source.at[part], result.at[part], sem.at[len(copies)]))
    for copy in copies:
        copy.start()
    for copy in copies:
        copy.wait()


def shards(grad_out, grad_side, attn_out, gate_pre, up_pre, seg_ids, down_weight, out_weight):
    vmem = pl.BlockSpec(memory_space=pltpu.VMEM)
    hbm = pl.BlockSpec(memory_space=pl.ANY)
    dma = pltpu.SemaphoreType.DMA
    shapes = tuple(
        jax.ShapeDtypeStruct(like.shape, BF16)
        for like in (gate_pre, up_pre, attn_out, down_weight, out_weight)
    )
    results = pl.pallas_call(
        kernel,
        out_shape=tuple(pltpu.VMEM(like.shape, BF16) for like in shapes),
        in_specs=[hbm] * 8,
        out_specs=(vmem,) * 5,
        scratch_shapes=[
            pltpu.VMEM((1, TOKENS), jnp.int32),
            pltpu.VMEM(grad_out.shape, BF16),
            pltpu.VMEM(grad_side.shape, BF16),
            pltpu.VMEM(attn_out.shape, BF16),
            pltpu.VMEM(gate_pre.shape, BF16),
            pltpu.VMEM(up_pre.shape, BF16),
            pltpu.VMEM((FF, WIDTH), BF16),
            pltpu.VMEM((AT, WIDTH), BF16),
            pltpu.VMEM((2, NZ, 4 * ROWS, WIDTH), BF16),
            pltpu.VMEM((4, ROWS, COLS), BF16),
            pltpu.VMEM((3, 4, ROWS, COLS), BF16),
            pltpu.VMEM((NZ, 4 * ROWS, COLS), BF16),
            pltpu.VMEM((COLS, TOKENS), BF16),
            pltpu.VMEM((NZ, 4 * ROWS, FF), BF16),
            pltpu.VMEM((NZ, 4 * ROWS, AT), BF16),
            pltpu.VMEM((2, 3, 4 * ROWS, FF), BF16),
            pltpu.VMEM((2, 3, 4 * ROWS, AT), BF16),
            pltpu.VMEM((2, 4 * ROWS, FF), BF16),
            pltpu.VMEM((2, 4 * ROWS, AT), BF16),
            pltpu.VMEM((8, ROWS, FF), BF16),
            pltpu.VMEM((8, ROWS, AT), BF16),
            dma((8,)),
            dma,
            dma((2, 2, 4, 2)),
            dma,
            dma((2, 8)),
            dma,
            dma((4,)),
            dma,
            dma((3,)),
            dma,
            dma((4, 2)),
            dma((2,)),
            dma((2, 2)),
            dma((2,)),
            dma((2,)),
        ],
        compiler_params=pltpu.CompilerParams(
            collective_id=0, has_side_effects=True, vmem_limit_bytes=56 * 2**20
        ),
        cost_estimate=pl.CostEstimate(
            flops=4 * TOKENS * WIDTH * COLS, bytes_accessed=20 * 2**20, transcendentals=0
        ),
    )(
        seg_ids.reshape(1, TOKENS), grad_out, grad_side, attn_out, gate_pre, up_pre,
        down_weight, out_weight,
    )
    return pl.pallas_call(
        copy_out,
        out_shape=shapes,
        in_specs=[vmem] * 5,
        out_specs=(hbm,) * 5,
        scratch_shapes=[dma((sum(PIECES),))],
        compiler_params=pltpu.CompilerParams(vmem_limit_bytes=20 * 2**20),
    )(*results)


def solution(mesh):
    return jax.shard_map(
        shards,
        mesh=mesh,
        in_specs=(
            P(("gx", "gy"), "gz"),
            P(("gx", "gy"), "gz"),
            P(("gx", "gz"), "gy"),
            P(("gx", "gz"), "gy"),
            P(("gx", "gz"), "gy"),
            P(),
            P(("gy", "gx"), "gz"),
            P(("gy", "gx"), "gz"),
        ),
        out_specs=(
            P(("gx", "gz"), "gy"),
            P(("gx", "gz"), "gy"),
            P(("gx", "gz"), "gy"),
            P(("gy", "gx"), "gz"),
            P(("gy", "gx"), "gz"),
        ),
        check_vma=False,
    )
```

```python
import jax
import jax.numpy as jnp
from jax import lax
from jax.experimental import pallas as pl
from jax.experimental.pallas import tpu as pltpu
from jax.sharding import PartitionSpec as P

NSEG = 8
MESH = pl.DeviceIdType.MESH
F32, BF16 = jnp.float32, jnp.bfloat16

NZ, NX = 8, 4
ROWS = 32
WIDTH = 2048
FF, AT = 832, 256
COLS = AT + FF
TOKENS = 1024
TILE = 256
TOP, BOTTOM = slice(0, 2 * ROWS), slice(2 * ROWS, 4 * ROWS)


def product_nt(lhs_mat, rhs_mat):
    return lax.dot_general(lhs_mat, rhs_mat, (((1,), (1,)), ((), ())), preferred_element_type=F32)


def kernel(
    seg_hbm, go_hbm, gs_hbm, attn_hbm, gate_hbm, up_hbm, dw_hbm, ow_hbm,
    ggate_ref, gup_ref, gattn_ref, dw_out, ow_out,
    seg_ref, go_ref, gs_ref, attn_ref, gate_ref, up_ref, dw, ow, grads, hsend, hx, hid, hid_t, part_f, part_a, mid, xin_f, xin_a, yout_f, yout_a, yin_f, yin_a,
    w_sem, zs, zr, ds, dr, ps, pr, h1s, h1r, h2s, h2r, c1s, c1r, c1m, c2s, c2r,
):
    gx, z, gz = lax.axis_index("gx"), lax.axis_index("gy"), lax.axis_index("gz")
    h, c, l, x = gx // 2, gx % 2, gz // NX, gz % NX
    weights, part, xin = (dw, ow), (part_f, part_a), (xin_f, xin_a)
    yout, yin = (yout_f, yout_a), (yin_f, yin_a)

    def at(hh, cc, zz, ll, xx):
        return (hh * 2 + cc, zz, ll * NX + xx)

    def send(src, dst, send_sem, recv_sem, device):
        copy = pltpu.make_async_remote_copy(
            src_ref=src, dst_ref=dst, send_sem=send_sem, recv_sem=recv_sem,
            device_id=device, device_id_type=MESH,
        )
        copy.start()

    def sent(ref, sem):
        pltpu.make_async_copy(ref, ref, sem).wait()

    came = sent

    column = [(dh, dc, dl) for dh in range(2) for dc in range(2) for dl in range(2)][1:]

    def in_column(offset):
        dh, dc, dl = offset
        return (h + dh) % 2, (c + dc) % 2, (l + dl) % 2

    right, left = at(h, c, (z + 1) % NZ, l, x), at(h, c, (z + NZ - 1) % NZ, l, x)
    core = at(h, 1 - c, z, l, x)
    across = at(1 - h, c, z, l, x)
    x_right, x_left = at(h, c, z, l, (x + 1) % NX), at(h, c, z, l, (x + NX - 1) % NX)

    barrier = pltpu.get_barrier_semaphore()
    peers = [right, left]
    for offset in column:
        hh, cc, ll = in_column(offset)
        peers.append(at(hh, cc, z, ll, x))
    for dx in range(1, NX):
        peers.append(at(h, c, z, l, (x + dx) % NX))
    for peer in peers:
        pl.semaphore_signal(barrier, inc=1, device_id=peer, device_id_type=MESH)

    fetches = [
        pltpu.make_async_copy(source, target, w_sem.at[i])
        for i, (source, target) in enumerate((
            (seg_hbm, seg_ref), (go_hbm, go_ref), (gs_hbm, gs_ref), (gate_hbm, gate_ref),
            (up_hbm, up_ref), (attn_hbm, attn_ref), (dw_hbm, dw), (ow_hbm, ow),
        ))
    ]
    for fetch in fetches:
        fetch.start()

    def rows_of(ref, cc, hh):
        return ref.at[pl.ds(pl.multiple_of((cc * 2 + hh) * ROWS, ROWS), ROWS)]

    def block(q, j, hh, cc=None):
        return rows_of(grads.at[q, j], c if cc is None else cc, hh)

    for fetch in fetches[:3]:
        fetch.wait()
    start = (gx * NZ + z) * ROWS
    seg = jnp.broadcast_to(seg_ref[...], (ROWS, TOKENS))
    token = lax.broadcasted_iota(jnp.int32, (ROWS, TOKENS), 1)
    row = lax.broadcasted_iota(jnp.int32, (ROWS, TOKENS), 0)
    own_id = jnp.sum(jnp.where(token == row + start, seg, 0), axis=1, keepdims=True)
    length = jnp.sum(jnp.where(seg == own_id, 1.0, 0.0).astype(F32), axis=1, keepdims=True)
    tok_weight = TOKENS / (NSEG * length)
    scaled = (tok_weight * go_ref[...].astype(F32)).astype(BF16)
    block(0, z, h)[...] = scaled
    block(1, z, h)[...] = (scaled.astype(F32) + gs_ref[...].astype(F32)).astype(BF16)

    def to_core(q, j, k, p):
        hh = h if p == 0 else 1 - h
        send(block(q, j, hh), block(q, j, hh), ds, dr.at[q, k], core)

    def to_z(q, direction, s, p, j):
        hh = h if p == 0 else 1 - h
        send(block(q, j, hh), block(q, j, hh), zs, zr.at[q, direction, s, p],
             right if direction == 0 else left)

    def from_core(q, j, k):
        came(grads.at[q, j, 0:2 * ROWS], dr.at[q, k])

    def from_z(q, direction, s, p, j):
        hh = h if p == 0 else 1 - h
        came(block(q, j, hh), zr.at[q, direction, s, p])

    pl.semaphore_wait(barrier, len(peers))

    def hid_block(ll, xx, cc, hh):
        return rows_of(hid.at[ll * NX + xx], cc, hh)

    def hidden_along_x():
        for dx in (1, 3, 2):
            send(hsend, hx.at[dx - 1], h1s, h1r.at[dx - 1], at(h, c, z, l, (x + NX - dx) % NX))

    def hidden_along_y(dx):
        source = hsend
        if dx:
            source = hx.at[dx - 1]
            came(source, h1r.at[dx - 1])
        xx = (x + dx) % NX
        for offset in column:
            if offset[0] <= offset[2]:
                hh, cc, ll = in_column(offset)
                send(source.at[hh * 2 + cc], hid_block(l, xx, c, h), h2s, h2r.at[dx, offset[0]],
                     at(hh, cc, z, ll, x))
        hid_block(l, xx, c, h)[...] = source[gx]

    def relay_hidden(dx):
        came(hid.at[0:2, 0:ROWS], h2r.at[dx, 1])
        for cc in range(2):
            rows = hid_block(1 - l, (x + dx) % NX, cc, 1 - h)
            send(rows, rows, h2s, h2r.at[dx, 0], at(h, c, z, 1 - l, x))

    def turn_hidden(dx):
        came(hid.at[0:5, 0:ROWS], h2r.at[dx, 0])
        for ll in range(2):
            j = ll * NX + (x + dx) % NX
            hid_t[:, pl.ds(pl.multiple_of(j * 4 * ROWS, 4 * ROWS), 4 * ROWS)] = hid[j].T

    send(block(0, z, h), block(0, z, h), ps, pr.at[0], across)
    to_z(0, 0, 0, 0, z)
    to_z(0, 1, 0, 0, z)
    to_core(0, z, 0, 0)
    for fetch in fetches[3:6]:
        fetch.wait()
    gate = gate_ref[...].astype(F32)
    up = up_ref[...].astype(F32)
    hidden = (gate * jax.nn.sigmoid(gate) * up).astype(BF16)
    for g in range(4):
        hsend[g, :, AT:COLS] = hidden[:, g * FF:(g + 1) * FF]
        hsend[g, :, 0:AT] = attn_ref[:, g * AT:(g + 1) * AT]
    hidden_along_x()
    to_z(1, 0, 0, 0, z)
    to_z(1, 1, 0, 0, z)
    came(block(0, z, 1 - h), pr.at[0])
    to_z(0, 0, 0, 1, z)
    to_z(0, 1, 0, 1, z)
    to_core(0, z, 0, 1)
    send(block(1, z, h), block(1, z, h), ps, pr.at[1], across)
    hidden_along_y(0)

    def product(q, j, k):
        from_core(q, j, k)
        part[q][j] = product_nt(grads[q, j], weights[q][...]).astype(BF16)
        part_on(q, j)

    def part_on(q, j):
        dx = (j + NX - x) % NX
        ll = j // NX
        if q == 1:

            @pl.when(dx != 0)
            def _():
                send(part_a.at[j], xin_a.at[ll, dx - 1], c1s.at[1], c1r.at[1, ll], at(h, c, z, l, j % NX))

            return

        @pl.when(dx == 2)
        def _():
            send(part_f.at[j, TOP], mid.at[0, ll], c1s.at[0], c1m.at[0, ll], x_right)
            send(part_f.at[j, BOTTOM], mid.at[1, ll], c1s.at[0], c1m.at[1, ll], x_left)

        @pl.when(dx == 1)
        def _():
            send(part_f.at[j, BOTTOM], xin_f.at[ll, 0, BOTTOM], c1s.at[0], c1r.at[0, ll], x_right)

        @pl.when(dx == 3)
        def _():
            send(part_f.at[j, TOP], xin_f.at[ll, 1, TOP], c1s.at[0], c1r.at[0, ll], x_left)

    def add_on(j):
        dx = (j + NX - x) % NX
        ll = j // NX

        def add(side, half, device):
            came(mid.at[side, ll], c1m.at[side, ll])
            total = part_f[j, half].astype(F32) + mid[side, ll].astype(F32)
            part_f[j, half] = total.astype(BF16)
            send(part_f.at[j, half], xin_f.at[ll, side, half], c1s.at[0], c1r.at[0, ll], device)

        pl.when(dx == 1)(lambda: add(0, TOP, x_right))
        pl.when(dx == 3)(lambda: add(1, BOTTOM, x_left))

    def add_ons(s):
        def one(direction, carry):
            add_on((z + NZ + (2 * direction - 1) * (1 + s)) % NZ)
            return carry

        lax.fori_loop(0, 2, one, 0)

    def beyond(direction, s):
        return (z + NZ - 1 - s) % NZ if direction == 0 else (z + 1 + s) % NZ

    def cross_resid():
        for direction in range(2):
            j = beyond(direction, 0)
            from_z(1, direction, 0, 0, j)
            send(block(1, j, h), block(1, j, h), ps, pr.at[2 + direction], across)
            to_core(1, j, 1 + direction, 0)

    def pass_half(q, s, p):
        for direction in range(2):
            j = beyond(direction, s)
            crossed = q == 1 and s == 0
            if crossed and p == 1:
                came(block(1, j, 1 - h), pr.at[2 + direction])
            elif not crossed:
                from_z(q, direction, s, p, j)
            if s < 2 or p == direction:
                to_z(q, direction, s + 1, p, j)
            if not crossed or p == 1:
                to_core(q, j, 1 + 2 * s + direction, p)

    def pass_on(q, s):
        for p in range(2):
            pass_half(q, s, p)

    def products(q, s):
        js = [beyond(direction, s) for direction in range(2)]
        for direction in range(2):
            from_core(q, js[direction], 1 + 2 * s + direction)
        both = jnp.concatenate([grads[q, j] for j in js], axis=0)
        both = product_nt(both, weights[q][...]).astype(BF16)
        for direction in range(2):
            part[q][js[direction]] = both[direction * 4 * ROWS:(direction + 1) * 4 * ROWS]

        def one(direction, carry):
            part_on(q, (z + NZ + (2 * direction - 1) * (1 + s)) % NZ)
            return carry

        lax.fori_loop(0, 2, one, 0)

    far = (z + 4) % NZ

    def pass_far(q):
        for p in range(2):
            from_z(q, p, 3, p, far)
            to_core(q, far, 7, p)

    def weight_grad(q, lo, hi):
        lhs, out = ((hid_t.at[AT:COLS], dw_out), (hid_t.at[0:AT], ow_out))[q]

        def one(t, carry):
            cols = pl.ds(pl.multiple_of(t * TILE, TILE), TILE)
            rows = grads[q, :, :, cols].reshape(TOKENS, TILE)
            out[:, cols] = jnp.dot(lhs[...], rows, preferred_element_type=F32).astype(BF16)
            return carry

        lax.fori_loop(lo, hi, one, 0)

    def sum_x(q, ll):
        came(xin[q].at[ll], c1r.at[q, ll])
        total = part[q][ll * NX + x].astype(F32)
        for i in range(xin[q].shape[1]):
            total = total + xin[q][ll, i].astype(F32)
        yout[q][ll] = total.astype(BF16)

    def send_y(q, ll):
        for dh, dc in ((0, 0), (0, 1), (1, 0), (1, 1)):
            hh, cc = (h + dh) % 2, (c + dc) % 2
            rows = rows_of(yout[q].at[ll], cc, hh)

            def away(rows=rows, hh=hh, cc=cc):
                send(rows, yin[q].at[gx * 2 + l], c2s.at[q], c2r.at[q], at(hh, cc, z, ll, x))

            if dh + dc:
                away()
            else:
                pl.when(ll != l)(away)

                @pl.when(ll == l)
                def _():
                    yin[q][gx * 2 + l] = rows[...]

    near = (x + NZ + 2 - z) % NZ // 5

    def sums_on(q, ll):
        sum_x(q, ll)
        send_y(q, ll)

    def summed(q):
        came(yin[q].at[0:7], c2r.at[q])
        return [yin[q][2 * g].astype(F32) + yin[q][2 * g + 1].astype(F32) for g in range(4)]

    pass_on(0, 0)
    for fetch in fetches[6:]:
        fetch.wait()
    cross_resid()
    product(0, z, 0)
    pass_half(0, 1, 0)
    products(0, 0)
    pass_half(0, 1, 1)
    relay_hidden(0)
    hidden_along_y(1)
    hidden_along_y(3)
    add_on(z)
    pass_half(0, 2, 0)
    products(0, 1)
    pass_half(0, 2, 1)
    came(block(1, z, 1 - h), pr.at[1])
    to_core(1, z, 0, 0)
    to_core(1, z, 0, 1)
    pass_on(1, 0)
    hidden_along_y(2)
    add_ons(0)
    products(0, 2)
    pass_far(0)
    relay_hidden(1)
    relay_hidden(3)
    add_ons(1)
    product(0, far, 7)
    product(1, z, 0)
    products(1, 0)
    pass_half(1, 1, 0)
    add_ons(2)
    pass_half(1, 1, 1)
    add_on(far)
    products(1, 1)
    relay_hidden(2)
    pass_half(1, 2, 0)
    turn_hidden(0)
    turn_hidden(1)
    sums_on(0, near)
    pass_half(1, 2, 1)
    products(1, 2)
    sums_on(0, 1 - near)
    turn_hidden(3)
    turn_hidden(2)
    sums_on(1, near)
    weight_grad(0, 0, 2)
    pass_far(1)
    product(1, far, 7)
    weight_grad(0, 2, 7)
    sums_on(1, 1 - near)
    weight_grad(0, 7, 8)
    weight_grad(1, 0, 8)

    grad_hidden = jnp.concatenate(summed(0), axis=1)
    gate = gate_ref[...].astype(F32)
    up = up_ref[...].astype(F32)
    sig = jax.nn.sigmoid(gate)
    ggate_ref[...] = (grad_hidden * up * sig * (1.0 + gate * (1.0 - sig))).astype(BF16)
    gup_ref[...] = (grad_hidden * gate * sig).astype(BF16)
    gattn_ref[...] = jnp.concatenate(summed(1), axis=1).astype(BF16)

    sent(grads.at[0, 0], ps)
    sent(grads.at[0, 0:6], zs)
    sent(grads.at[0, 0, 0:2 * ROWS], zs)
    sent(grads.at[0], ds)
    sent(hx, h1s)
    sent(hid.at[0:7], h2s)
    for q in range(2):
        sent(part[q].at[0:6], c1s.at[q])
        sent(yin[q].at[0:7], c2s.at[q])


PIECES = (1, 1, 1, 4, 2)


def copy_out(*refs):
    sources, results, sem = refs[:5], refs[5:10], refs[10]
    copies = []
    for source, result, pieces in zip(sources, results, PIECES):
        rows = source.shape[0] // pieces
        for i in range(pieces):
            part = pl.ds(i * rows, rows)
            copies.append(pltpu.make_async_copy(source.at[part], result.at[part], sem.at[len(copies)]))
    for copy in copies:
        copy.start()
    for copy in copies:
        copy.wait()


def shards(grad_out, grad_side, attn_out, gate_pre, up_pre, seg_ids, down_weight, out_weight):
    vmem = pl.BlockSpec(memory_space=pltpu.VMEM)
    hbm = pl.BlockSpec(memory_space=pl.ANY)
    dma = pltpu.SemaphoreType.DMA
    shapes = tuple(
        jax.ShapeDtypeStruct(like.shape, BF16)
        for like in (gate_pre, up_pre, attn_out, down_weight, out_weight)
    )
    results = pl.pallas_call(
        kernel,
        out_shape=tuple(pltpu.VMEM(like.shape, BF16) for like in shapes),
        in_specs=[hbm] * 8,
        out_specs=(vmem,) * 5,
        scratch_shapes=[
            pltpu.VMEM((1, TOKENS), jnp.int32),
            pltpu.VMEM(grad_out.shape, BF16),
            pltpu.VMEM(grad_side.shape, BF16),
            pltpu.VMEM(attn_out.shape, BF16),
            pltpu.VMEM(gate_pre.shape, BF16),
            pltpu.VMEM(up_pre.shape, BF16),
            pltpu.VMEM((FF, WIDTH), BF16),
            pltpu.VMEM((AT, WIDTH), BF16),
            pltpu.VMEM((2, NZ, 4 * ROWS, WIDTH), BF16),
            pltpu.VMEM((4, ROWS, COLS), BF16),
            pltpu.VMEM((3, 4, ROWS, COLS), BF16),
            pltpu.VMEM((NZ, 4 * ROWS, COLS), BF16),
            pltpu.VMEM((COLS, TOKENS), BF16),
            pltpu.VMEM((NZ, 4 * ROWS, FF), BF16),
            pltpu.VMEM((NZ, 4 * ROWS, AT), BF16),
            pltpu.VMEM((2, 2, 2 * ROWS, FF), BF16),
            pltpu.VMEM((2, 2, 4 * ROWS, FF), BF16),
            pltpu.VMEM((2, 3, 4 * ROWS, AT), BF16),
            pltpu.VMEM((2, 4 * ROWS, FF), BF16),
            pltpu.VMEM((2, 4 * ROWS, AT), BF16),
            pltpu.VMEM((8, ROWS, FF), BF16),
            pltpu.VMEM((8, ROWS, AT), BF16),
            dma((8,)),
            dma,
            dma((2, 2, 4, 2)),
            dma,
            dma((2, 8)),
            dma,
            dma((4,)),
            dma,
            dma((3,)),
            dma,
            dma((4, 2)),
            dma((2,)),
            dma((2, 2)),
            dma((2, 2)),
            dma((2,)),
            dma((2,)),
        ],
        compiler_params=pltpu.CompilerParams(
            collective_id=0, has_side_effects=True, vmem_limit_bytes=56 * 2**20
        ),
        cost_estimate=pl.CostEstimate(
            flops=4 * TOKENS * WIDTH * COLS, bytes_accessed=20 * 2**20, transcendentals=0
        ),
    )(
        seg_ids.reshape(1, TOKENS), grad_out, grad_side, attn_out, gate_pre, up_pre,
        down_weight, out_weight,
    )
    return pl.pallas_call(
        copy_out,
        out_shape=shapes,
        in_specs=[vmem] * 5,
        out_specs=(hbm,) * 5,
        scratch_shapes=[dma((sum(PIECES),))],
        compiler_params=pltpu.CompilerParams(vmem_limit_bytes=20 * 2**20),
    )(*results)


def solution(mesh):
    return jax.shard_map(
        shards,
        mesh=mesh,
        in_specs=(
            P(("gx", "gy"), "gz"),
            P(("gx", "gy"), "gz"),
            P(("gx", "gz"), "gy"),
            P(("gx", "gz"), "gy"),
            P(("gx", "gz"), "gy"),
            P(),
            P(("gy", "gx"), "gz"),
            P(("gy", "gx"), "gz"),
        ),
        out_specs=(
            P(("gx", "gz"), "gy"),
            P(("gx", "gz"), "gy"),
            P(("gx", "gz"), "gy"),
            P(("gy", "gx"), "gz"),
            P(("gy", "gx"), "gz"),
        ),
        check_vma=False,
    )
```

```python
import jax
import jax.numpy as jnp
from jax import lax
from jax.experimental import pallas as pl
from jax.experimental.pallas import tpu as pltpu
from jax.sharding import PartitionSpec as P

NSEG = 8
MESH = pl.DeviceIdType.MESH
F32, BF16 = jnp.float32, jnp.bfloat16

NZ, NX = 8, 4
ROWS = 32
WIDTH = 2048
FF, AT = 832, 256
COLS = AT + FF
TOKENS = 1024
TILE = 512
TOP, BOTTOM = slice(0, 2 * ROWS), slice(2 * ROWS, 4 * ROWS)


def product_nt(lhs_mat, rhs_mat):
    return lax.dot_general(lhs_mat, rhs_mat, (((1,), (1,)), ((), ())), preferred_element_type=F32)


def kernel(
    seg_hbm, go_hbm, gs_hbm, attn_hbm, gate_hbm, up_hbm, dw_hbm, ow_hbm,
    ggate_ref, gup_ref, gattn_ref, dw_out, ow_out,
    seg_ref, go_ref, gs_ref, attn_ref, gate_ref, up_ref, gate_factor, up_factor, dw, ow, grads, hsend, hx, hid, hid_t, part_f, part_a, mid, xin_f, xin_a, yout_f, yout_a, yin_f, yin_a,
    w_sem, zs, zr, ds, dr, ps, pr, h1s, h1r, h2s, h2r, c1s, c1r, c1m, c2s, c2r,
):
    gx, z, gz = lax.axis_index("gx"), lax.axis_index("gy"), lax.axis_index("gz")
    h, c, l, x = gx // 2, gx % 2, gz // NX, gz % NX
    weights, part, xin = (dw, ow), (part_f, part_a), (xin_f, xin_a)
    yout, yin = (yout_f, yout_a), (yin_f, yin_a)

    def at(hh, cc, zz, ll, xx):
        return (hh * 2 + cc, zz, ll * NX + xx)

    def send(src, dst, send_sem, recv_sem, device):
        copy = pltpu.make_async_remote_copy(
            src_ref=src, dst_ref=dst, send_sem=send_sem, recv_sem=recv_sem,
            device_id=device, device_id_type=MESH,
        )
        copy.start()

    def sent(ref, sem):
        pltpu.make_async_copy(ref, ref, sem).wait()

    came = sent

    column = [(dh, dc, dl) for dh in range(2) for dc in range(2) for dl in range(2)][1:]

    def in_column(offset):
        dh, dc, dl = offset
        return (h + dh) % 2, (c + dc) % 2, (l + dl) % 2

    right, left = at(h, c, (z + 1) % NZ, l, x), at(h, c, (z + NZ - 1) % NZ, l, x)
    core = at(h, 1 - c, z, l, x)
    across = at(1 - h, c, z, l, x)
    x_right, x_left = at(h, c, z, l, (x + 1) % NX), at(h, c, z, l, (x + NX - 1) % NX)

    barrier = pltpu.get_barrier_semaphore()
    peers = [right, left]
    for offset in column:
        hh, cc, ll = in_column(offset)
        peers.append(at(hh, cc, z, ll, x))
    for dx in range(1, NX):
        peers.append(at(h, c, z, l, (x + dx) % NX))
    for peer in peers:
        pl.semaphore_signal(barrier, inc=1, device_id=peer, device_id_type=MESH)

    fetches = [
        pltpu.make_async_copy(source, target, w_sem.at[i])
        for i, (source, target) in enumerate((
            (seg_hbm, seg_ref), (go_hbm, go_ref), (gs_hbm, gs_ref), (gate_hbm, gate_ref),
            (up_hbm, up_ref), (attn_hbm, attn_ref), (dw_hbm, dw), (ow_hbm, ow),
        ))
    ]
    for fetch in fetches:
        fetch.start()

    def rows_of(ref, cc, hh):
        return ref.at[pl.ds(pl.multiple_of((cc * 2 + hh) * ROWS, ROWS), ROWS)]

    def block(q, j, hh, cc=None):
        return rows_of(grads.at[q, j], c if cc is None else cc, hh)

    for fetch in fetches[:3]:
        fetch.wait()
    start = (gx * NZ + z) * ROWS
    seg = jnp.broadcast_to(seg_ref[...], (ROWS, TOKENS))
    token = lax.broadcasted_iota(jnp.int32, (ROWS, TOKENS), 1)
    row = lax.broadcasted_iota(jnp.int32, (ROWS, TOKENS), 0)
    own_id = jnp.sum(jnp.where(token == row + start, seg, 0), axis=1, keepdims=True)
    length = jnp.sum(jnp.where(seg == own_id, 1.0, 0.0).astype(F32), axis=1, keepdims=True)
    tok_weight = TOKENS / (NSEG * length)
    scaled = (tok_weight * go_ref[...].astype(F32)).astype(BF16)
    block(0, z, h)[...] = scaled
    block(1, z, h)[...] = (scaled.astype(F32) + gs_ref[...].astype(F32)).astype(BF16)

    def to_core(q, j, k, p):
        hh = h if p == 0 else 1 - h
        send(block(q, j, hh), block(q, j, hh), ds, dr.at[q, k], core)

    def to_z(q, direction, s, p, j):
        hh = h if p == 0 else 1 - h
        send(block(q, j, hh), block(q, j, hh), zs, zr.at[q, direction, s, p],
             right if direction == 0 else left)

    def from_core(q, j, k):
        came(grads.at[q, j, 0:2 * ROWS], dr.at[q, k])

    def from_z(q, direction, s, p, j):
        hh = h if p == 0 else 1 - h
        came(block(q, j, hh), zr.at[q, direction, s, p])

    pl.semaphore_wait(barrier, len(peers))

    def hid_block(ll, xx, cc, hh):
        return rows_of(hid.at[ll * NX + xx], cc, hh)

    def hidden_along_x():
        for dx in (1, 3, 2):
            send(hsend, hx.at[dx - 1], h1s, h1r.at[dx - 1], at(h, c, z, l, (x + NX - dx) % NX))

    def hidden_along_y(dx):
        source = hsend
        if dx:
            source = hx.at[dx - 1]
            came(source, h1r.at[dx - 1])
        xx = (x + dx) % NX
        for offset in column:
            if offset[0] <= offset[2]:
                hh, cc, ll = in_column(offset)
                send(source.at[hh * 2 + cc], hid_block(l, xx, c, h), h2s, h2r.at[dx, offset[0]],
                     at(hh, cc, z, ll, x))
        hid_block(l, xx, c, h)[...] = source[gx]

    def relay_hidden(dx):
        came(hid.at[0:2, 0:ROWS], h2r.at[dx, 1])
        for cc in range(2):
            rows = hid_block(1 - l, (x + dx) % NX, cc, 1 - h)
            send(rows, rows, h2s, h2r.at[dx, 0], at(h, c, z, 1 - l, x))

    def turn_hidden(dx):
        came(hid.at[0:5, 0:ROWS], h2r.at[dx, 0])
        for ll in range(2):
            j = ll * NX + (x + dx) % NX
            hid_t[:, pl.ds(pl.multiple_of(j * 4 * ROWS, 4 * ROWS), 4 * ROWS)] = hid[j].T

    send(block(0, z, h), block(0, z, h), ps, pr.at[0], across)
    to_z(0, 0, 0, 0, z)
    to_z(0, 1, 0, 0, z)
    to_core(0, z, 0, 0)
    for fetch in fetches[3:6]:
        fetch.wait()
    gate = gate_ref[...].astype(F32)
    up = up_ref[...].astype(F32)
    sig = jax.nn.sigmoid(gate)
    silu = gate * sig
    hidden = (silu * up).astype(BF16)
    up_factor[...] = silu
    gate_factor[...] = up * sig * (1.0 + gate * (1.0 - sig))
    for g in range(4):
        hsend[g, :, AT:COLS] = hidden[:, g * FF:(g + 1) * FF]
        hsend[g, :, 0:AT] = attn_ref[:, g * AT:(g + 1) * AT]
    hidden_along_x()
    to_z(1, 0, 0, 0, z)
    to_z(1, 1, 0, 0, z)
    came(block(0, z, 1 - h), pr.at[0])
    to_z(0, 0, 0, 1, z)
    to_z(0, 1, 0, 1, z)
    to_core(0, z, 0, 1)
    send(block(1, z, h), block(1, z, h), ps, pr.at[1], across)
    hidden_along_y(0)

    def product(q, j, k):
        from_core(q, j, k)
        part[q][j] = product_nt(grads[q, j], weights[q][...]).astype(BF16)
        part_on(q, j)

    def part_on(q, j):
        dx = (j + NX - x) % NX
        ll = j // NX
        if q == 1:

            @pl.when(dx != 0)
            def _():
                send(part_a.at[j], xin_a.at[ll, dx - 1], c1s.at[1], c1r.at[1, ll], at(h, c, z, l, j % NX))

            return

        @pl.when(dx == 2)
        def _():
            send(part_f.at[j, TOP], mid.at[0, ll], c1s.at[0], c1m.at[0, ll], x_right)
            send(part_f.at[j, BOTTOM], mid.at[1, ll], c1s.at[0], c1m.at[1, ll], x_left)

        @pl.when(dx == 1)
        def _():
            send(part_f.at[j, BOTTOM], xin_f.at[ll, 0, BOTTOM], c1s.at[0], c1r.at[0, ll], x_right)

        @pl.when(dx == 3)
        def _():
            send(part_f.at[j, TOP], xin_f.at[ll, 1, TOP], c1s.at[0], c1r.at[0, ll], x_left)

    def add_on(j):
        dx = (j + NX - x) % NX
        ll = j // NX

        def add(side, half, device):
            came(mid.at[side, ll], c1m.at[side, ll])
            total = part_f[j, half].astype(F32) + mid[side, ll].astype(F32)
            part_f[j, half] = total.astype(BF16)
            send(part_f.at[j, half], xin_f.at[ll, side, half], c1s.at[0], c1r.at[0, ll], device)

        pl.when(dx == 1)(lambda: add(0, TOP, x_right))
        pl.when(dx == 3)(lambda: add(1, BOTTOM, x_left))

    def add_ons(s):
        def one(direction, carry):
            add_on((z + NZ + (2 * direction - 1) * (1 + s)) % NZ)
            return carry

        lax.fori_loop(0, 2, one, 0)

    def beyond(direction, s):
        return (z + NZ - 1 - s) % NZ if direction == 0 else (z + 1 + s) % NZ

    def cross_resid():
        for direction in range(2):
            j = beyond(direction, 0)
            from_z(1, direction, 0, 0, j)
            send(block(1, j, h), block(1, j, h), ps, pr.at[2 + direction], across)
            to_core(1, j, 1 + direction, 0)

    def pass_half(q, s, p):
        for direction in range(2):
            j = beyond(direction, s)
            crossed = q == 1 and s == 0
            if crossed and p == 1:
                came(block(1, j, 1 - h), pr.at[2 + direction])
            elif not crossed:
                from_z(q, direction, s, p, j)
            if s < 2 or p == direction:
                to_z(q, direction, s + 1, p, j)
            if not crossed or p == 1:
                to_core(q, j, 1 + 2 * s + direction, p)

    def pass_on(q, s):
        for p in range(2):
            pass_half(q, s, p)

    def products(q, s):
        js = [beyond(direction, s) for direction in range(2)]
        for direction in range(2):
            from_core(q, js[direction], 1 + 2 * s + direction)
        both = jnp.concatenate([grads[q, j] for j in js], axis=0)
        both = product_nt(both, weights[q][...]).astype(BF16)
        for direction in range(2):
            part[q][js[direction]] = both[direction * 4 * ROWS:(direction + 1) * 4 * ROWS]

        def one(direction, carry):
            part_on(q, (z + NZ + (2 * direction - 1) * (1 + s)) % NZ)
            return carry

        lax.fori_loop(0, 2, one, 0)

    far = (z + 4) % NZ

    def pass_far(q):
        for p in range(2):
            from_z(q, p, 3, p, far)
            to_core(q, far, 7, p)

    def weight_grad(q, lo, hi):
        lhs, out = ((hid_t.at[AT:COLS], dw_out), (hid_t.at[0:AT], ow_out))[q]

        def one(t, carry):
            cols = pl.ds(pl.multiple_of(t * TILE, TILE), TILE)
            rows = grads[q, :, :, cols].reshape(TOKENS, TILE)
            out[:, cols] = jnp.dot(lhs[...], rows, preferred_element_type=F32).astype(BF16)
            return carry

        lax.fori_loop(lo, hi, one, 0)

    def sum_x(q, ll):
        came(xin[q].at[ll], c1r.at[q, ll])
        total = part[q][ll * NX + x].astype(F32)
        for i in range(xin[q].shape[1]):
            total = total + xin[q][ll, i].astype(F32)
        yout[q][ll] = total.astype(BF16)

    def send_y(q, ll):
        for dh, dc in ((0, 0), (0, 1), (1, 0), (1, 1)):
            hh, cc = (h + dh) % 2, (c + dc) % 2
            rows = rows_of(yout[q].at[ll], cc, hh)

            def away(rows=rows, hh=hh, cc=cc):
                send(rows, yin[q].at[gx * 2 + l], c2s.at[q], c2r.at[q], at(hh, cc, z, ll, x))

            if dh + dc:
                away()
            else:
                pl.when(ll != l)(away)

                @pl.when(ll == l)
                def _():
                    yin[q][gx * 2 + l] = rows[...]

    near = (x + NZ + 2 - z) % NZ // 5

    def sums_on(q, ll):
        sum_x(q, ll)
        send_y(q, ll)

    def summed(q):
        came(yin[q].at[0:7], c2r.at[q])
        return [yin[q][2 * g].astype(F32) + yin[q][2 * g + 1].astype(F32) for g in range(4)]

    pass_on(0, 0)
    for fetch in fetches[6:]:
        fetch.wait()
    cross_resid()
    product(0, z, 0)
    pass_half(0, 1, 0)
    products(0, 0)
    pass_half(0, 1, 1)
    relay_hidden(0)
    hidden_along_y(1)
    hidden_along_y(3)
    add_on(z)
    pass_half(0, 2, 0)
    products(0, 1)
    pass_half(0, 2, 1)
    came(block(1, z, 1 - h), pr.at[1])
    to_core(1, z, 0, 0)
    to_core(1, z, 0, 1)
    pass_on(1, 0)
    hidden_along_y(2)
    add_ons(0)
    products(0, 2)
    pass_far(0)
    relay_hidden(1)
    relay_hidden(3)
    add_ons(1)
    product(0, far, 7)
    product(1, z, 0)
    products(1, 0)
    pass_half(1, 1, 0)
    add_ons(2)
    turn_hidden(0)
    pass_half(1, 1, 1)
    add_on(far)
    products(1, 1)
    relay_hidden(2)
    turn_hidden(1)
    pass_half(1, 2, 0)
    turn_hidden(3)
    turn_hidden(2)
    sums_on(0, near)
    weight_grad(0, 0, 1)
    pass_half(1, 2, 1)
    products(1, 2)
    sums_on(0, 1 - near)
    sums_on(1, near)
    weight_grad(0, 1, 2)
    pass_far(1)
    product(1, far, 7)
    weight_grad(0, 2, 4)
    sums_on(1, 1 - near)
    weight_grad(1, 0, 4)

    grad_hidden = jnp.concatenate(summed(0), axis=1)
    ggate_ref[...] = (grad_hidden * gate_factor[...]).astype(BF16)
    gup_ref[...] = (grad_hidden * up_factor[...]).astype(BF16)
    gattn_ref[...] = jnp.concatenate(summed(1), axis=1).astype(BF16)

    sent(grads.at[0, 0], ps)
    sent(grads.at[0, 0:6], zs)
    sent(grads.at[0, 0, 0:2 * ROWS], zs)
    sent(grads.at[0], ds)
    sent(hx, h1s)
    sent(hid.at[0:7], h2s)
    for q in range(2):
        sent(part[q].at[0:6], c1s.at[q])
        sent(yin[q].at[0:7], c2s.at[q])


PIECES = (1, 1, 1, 4, 2)


def copy_out(*refs):
    sources, results, sem = refs[:5], refs[5:10], refs[10]
    copies = []
    for source, result, pieces in zip(sources, results, PIECES):
        rows = source.shape[0] // pieces
        for i in range(pieces):
            part = pl.ds(i * rows, rows)
            copies.append(pltpu.make_async_copy(source.at[part], result.at[part], sem.at[len(copies)]))
    for copy in copies:
        copy.start()
    for copy in copies:
        copy.wait()


def shards(grad_out, grad_side, attn_out, gate_pre, up_pre, seg_ids, down_weight, out_weight):
    vmem = pl.BlockSpec(memory_space=pltpu.VMEM)
    hbm = pl.BlockSpec(memory_space=pl.ANY)
    dma = pltpu.SemaphoreType.DMA
    shapes = tuple(
        jax.ShapeDtypeStruct(like.shape, BF16)
        for like in (gate_pre, up_pre, attn_out, down_weight, out_weight)
    )
    results = pl.pallas_call(
        kernel,
        out_shape=tuple(pltpu.VMEM(like.shape, BF16) for like in shapes),
        in_specs=[hbm] * 8,
        out_specs=(vmem,) * 5,
        scratch_shapes=[
            pltpu.VMEM((1, TOKENS), jnp.int32),
            pltpu.VMEM(grad_out.shape, BF16),
            pltpu.VMEM(grad_side.shape, BF16),
            pltpu.VMEM(attn_out.shape, BF16),
            pltpu.VMEM(gate_pre.shape, BF16),
            pltpu.VMEM(up_pre.shape, BF16),
            pltpu.VMEM(gate_pre.shape, F32),
            pltpu.VMEM(up_pre.shape, F32),
            pltpu.VMEM((FF, WIDTH), BF16),
            pltpu.VMEM((AT, WIDTH), BF16),
            pltpu.VMEM((2, NZ, 4 * ROWS, WIDTH), BF16),
            pltpu.VMEM((4, ROWS, COLS), BF16),
            pltpu.VMEM((3, 4, ROWS, COLS), BF16),
            pltpu.VMEM((NZ, 4 * ROWS, COLS), BF16),
            pltpu.VMEM((COLS, TOKENS), BF16),
            pltpu.VMEM((NZ, 4 * ROWS, FF), BF16),
            pltpu.VMEM((NZ, 4 * ROWS, AT), BF16),
            pltpu.VMEM((2, 2, 2 * ROWS, FF), BF16),
            pltpu.VMEM((2, 2, 4 * ROWS, FF), BF16),
            pltpu.VMEM((2, 3, 4 * ROWS, AT), BF16),
            pltpu.VMEM((2, 4 * ROWS, FF), BF16),
            pltpu.VMEM((2, 4 * ROWS, AT), BF16),
            pltpu.VMEM((8, ROWS, FF), BF16),
            pltpu.VMEM((8, ROWS, AT), BF16),
            dma((8,)),
            dma,
            dma((2, 2, 4, 2)),
            dma,
            dma((2, 8)),
            dma,
            dma((4,)),
            dma,
            dma((3,)),
            dma,
            dma((4, 2)),
            dma((2,)),
            dma((2, 2)),
            dma((2, 2)),
            dma((2,)),
            dma((2,)),
        ],
        compiler_params=pltpu.CompilerParams(
            collective_id=0, has_side_effects=True, vmem_limit_bytes=56 * 2**20
        ),
        cost_estimate=pl.CostEstimate(
            flops=4 * TOKENS * WIDTH * COLS, bytes_accessed=20 * 2**20, transcendentals=0
        ),
    )(
        seg_ids.reshape(1, TOKENS), grad_out, grad_side, attn_out, gate_pre, up_pre,
        down_weight, out_weight,
    )
    return pl.pallas_call(
        copy_out,
        out_shape=shapes,
        in_specs=[vmem] * 5,
        out_specs=(hbm,) * 5,
        scratch_shapes=[dma((sum(PIECES),))],
        compiler_params=pltpu.CompilerParams(vmem_limit_bytes=20 * 2**20),
    )(*results)


def solution(mesh):
    return jax.shard_map(
        shards,
        mesh=mesh,
        in_specs=(
            P(("gx", "gy"), "gz"),
            P(("gx", "gy"), "gz"),
            P(("gx", "gz"), "gy"),
            P(("gx", "gz"), "gy"),
            P(("gx", "gz"), "gy"),
            P(),
            P(("gy", "gx"), "gz"),
            P(("gy", "gx"), "gz"),
        ),
        out_specs=(
            P(("gx", "gz"), "gy"),
            P(("gx", "gz"), "gy"),
            P(("gx", "gz"), "gy"),
            P(("gy", "gx"), "gz"),
            P(("gy", "gx"), "gz"),
        ),
        check_vma=False,
    )
```
